128 devices in a mesh: lat: 4 (over z), lon: 32 (over y, x, core).
Axes of the slice: x: 4, y: 4, z: 4, core: 2. Of those that a mesh axis runs over, the one named last changes fastest.
Arguments:
- latents: bfloat16 [32768, 512], P(('lat', 'lon')), may hold values from -6 to 6
- near_index: int32 [4, 32768], P(None, ('lat', 'lon')), may hold values from 0 to 511
- coarse_slot: int32 [2, 32768], P(None, ('lat', 'lon')), may hold values from 0 to 1023, as said below
- coarse_send: int32 [128, 1024], P(('lat', 'lon')), may hold values from 0 to 255
- norm_gain: float32 [512], replicated, may hold values from 0.1 to 1.9
- send_weight: bfloat16 [512, 512], replicated, may hold values from -0.25 to 0.25
- receive_weight: bfloat16 [512, 512], replicated, may hold values from -0.25 to 0.25
- edge_bias: float32 [512], replicated, may hold values from -3 to 3
- edge_weight: bfloat16 [512, 512], replicated, may hold values from -0.25 to 0.25
- edge_gain: float32 [512], replicated, may hold values from 0.1 to 1.9
- node_input: bfloat16 [1024, 512], replicated, may hold values from -0.1875 to 0.1875
- node_bias: float32 [512], replicated, may hold values from -3 to 3
- node_output: bfloat16 [512, 512], replicated, may hold values from -0.25 to 0.25
- cotangent: bfloat16 [32768, 512], P(('lat', 'lon')), may hold values from -6 to 6
Outputs:
- new_latents: bfloat16 [32768, 512], P(('lat', 'lon'))
- grad_latents: bfloat16 [32768, 512], P(('lat', 'lon'))
- grad_send: float32 [512, 512], replicated
- grad_receive: float32 [512, 512], replicated
- grad_edge: float32 [512, 512], replicated
- grad_node_input: float32 [1024, 512], replicated
- grad_node_output: float32 [512, 512], replicated
- grad_vectors: float32 [4, 512], replicated
The draws below stay inside these ranges and needn't reach their ends.
Inputs may be any that keep to these rules, and one draw needn't show every extreme that they name: `coarse_slot`: on each device the 512 coarse edges name distinct slots. Slot s is position s % 8 among the rows that source device s // 8 (lat-major) sends to this device, so at most 8 of one device's coarse edges come from one source device.
All inputs are finite; a program needn't handle non-finite values.
Results may differ from the reference program's by a relative error of at most 0.012.
Values may be sent and summed in bfloat16 or wider, within the bound.
A program may use at most 64 MiB of HBM per device.

```python
import jax
import jax.numpy as jnp
from jax import lax

D = 512
ROWS_DEV = 256
DEG = 4
CDEG = 2
RIM = 128
NODES = 32768
PAIR_CAP = 8
SLOTS = 1024
N_LAT = 4
N_LON = 32


def draw_coarse_slot(key, part):
    key = jax.random.fold_in(key, 7)
    devices = N_LAT * N_LON
    slot_count = devices * PAIR_CAP

    def one_device(device_key):
        key_factor, key_forced, key_jitter, key_order = jax.random.split(device_key, 4)
        factor = jax.random.randint(key_factor, (devices,), 1, 9)
        forced = jax.random.randint(key_forced, (), 0, devices)
        factor = jnp.where(jnp.arange(devices) == forced, 0, factor)
        jitter = jax.random.randint(key_jitter, (devices, PAIR_CAP), 0, 4096)
        scores = (jitter * factor[:, None]).reshape(slot_count) * 8192 + jnp.arange(slot_count)
        edge_slots = jnp.arange(slot_count)
        scores = jnp.where((edge_slots == 0) | (edge_slots == slot_count - 1), -1 - edge_slots, scores)
        chosen = jnp.argsort(scores)[:CDEG * ROWS_DEV]
        chosen = jax.random.permutation(key_order, chosen)
        return chosen.reshape(CDEG, ROWS_DEV)
    device_keys = jax.random.split(key, devices)
    picked = jax.vmap(one_device)(device_keys)
    return jnp.transpose(picked, (1, 0, 2)).reshape(CDEG, devices * ROWS_DEV).astype(jnp.int32)


def set_ends(drawn, stream_key, smallest, largest):
    longest = drawn.shape.index(max(drawn.shape))
    spots = []
    for shift in (0, 1):
        where = [jax.random.randint(jax.random.fold_in(stream_key, axis), (), 0, length) for axis, length in enumerate(drawn.shape)]
        where[longest] = (where[longest] + shift) % drawn.shape[longest]
        spots.append(tuple(where))
    return drawn.at[spots[0]].set(smallest).at[spots[1]].set(largest)


def block_scale(rng, dims, cuts, least, largest):
    def one(dim, shards_of):
        steps = jax.random.uniform(jax.random.fold_in(jax.random.fold_in(rng, 6), dim), (shards_of,), jnp.float32, least / len(cuts), largest / len(cuts))
        return jnp.repeat(jnp.exp(steps), dims[dim] // shards_of).reshape((-1,) + (1,) * (len(dims) - dim - 1))

    factor_of = one(*cuts[0])
    for cut in cuts[1:]:
        factor_of = factor_of * one(*cut)
    return factor_of


def normal_values(stream_key, shape, scale, most, cuts=(), dtype=jnp.bfloat16):
    drawn = scale * jax.random.normal(stream_key, shape, jnp.float32)
    if cuts:
        drawn = drawn * block_scale(stream_key, shape, cuts, -0.22, 0.18)
    return jnp.clip(drawn, -most, most).astype(dtype)


def setup_inputs(seed: int = 0) -> dict:
    seeds = jax.random.split(jax.random.key(seed), 15)
    return {
        "latents": normal_values(seeds[0], (NODES, D), 1.0, 6.0, ((0, 128),)),
        "near_index": set_ends(jax.random.randint(seeds[1], (DEG, NODES), 0, ROWS_DEV + 2 * RIM), jax.random.fold_in(seeds[1], 1), 0, (ROWS_DEV + 2 * RIM) - 1).astype(jnp.int32),
        "coarse_slot": draw_coarse_slot(jax.random.fold_in(seeds[14], 71), 0),
        "coarse_send": set_ends(jax.random.randint(seeds[3], (N_LAT * N_LON, SLOTS), 0, ROWS_DEV), jax.random.fold_in(seeds[3], 1), 0, ROWS_DEV - 1).astype(jnp.int32),
        "norm_gain": jnp.clip(1.0 + 0.18 * jax.random.normal(seeds[4], (D,), jnp.float32), 0.1, 1.9),
        "send_weight": normal_values(seeds[5], (D, D), D ** -0.5, 0.25),
        "receive_weight": normal_values(seeds[6], (D, D), D ** -0.5, 0.25),
        "edge_bias": normal_values(seeds[7], (D,), 0.5, 3.0, (), jnp.float32),
        "edge_weight": normal_values(seeds[8], (D, D), D ** -0.5, 0.25),
        "edge_gain": jnp.clip(1.0 + 0.18 * jax.random.normal(seeds[9], (D,), jnp.float32), 0.1, 1.9),
        "node_input": normal_values(seeds[10], (2 * D, D), (2 * D) ** -0.5, 0.1875),
        "node_bias": normal_values(seeds[11], (D,), 0.5, 3.0, (), jnp.float32),
        "node_output": normal_values(seeds[12], (D, D), D ** -0.5, 0.25),
        "cotangent": normal_values(seeds[13], (NODES, D), 1.0, 6.0, ((0, 128),)),
    }


EPS = 1e-05

def norm_rows(values):
    centred = values - lax.optimization_barrier(jnp.mean(values, axis=-1, keepdims=True))
    inverse = lax.rsqrt(lax.optimization_barrier(jnp.mean(centred * centred, axis=-1, keepdims=True)) + EPS)
    return (centred * inverse, inverse)

def norm_back(upstream, normalized, inverse):
    return (upstream - lax.optimization_barrier(jnp.mean(upstream, axis=-1, keepdims=True)) - normalized * lax.optimization_barrier(jnp.mean(upstream * normalized, axis=-1, keepdims=True))) * inverse

def silu_slope(values):
    logistic = jax.nn.sigmoid(values)
    return logistic * (1.0 + values * (1.0 - logistic))

def outer_sum(former, latter):
    return lax.dot_general(former, latter, (((0,), (0,)), ((), ())), preferred_element_type=jnp.float32)

def back_dot(former, latter):
    return lax.dot_general(former, latter, (((1,), (1,)), ((), ())), preferred_element_type=jnp.float32)

def edge_node_pass(latents, normed, receive_part, senders, receive_weight, edge_weight, edge_gain, node_input, node_bias, node_output, cotangent):
    edge_count, row_count, feature = senders.shape
    edge_in = senders.astype(jnp.float32) + receive_part[None]
    activated = jax.nn.silu(edge_in).astype(jnp.bfloat16)
    flat_active = activated.reshape(edge_count * row_count, feature)
    edge_pre = jnp.dot(flat_active, edge_weight, preferred_element_type=jnp.float32)
    edge_hat, edge_inv = norm_rows(edge_pre)
    edge_hat = edge_hat.reshape(edge_count, row_count, feature)
    edge_inv = edge_inv.reshape(edge_count, row_count, 1)
    aggregate = lax.optimization_barrier(jnp.sum(edge_hat * edge_gain, axis=0)).astype(jnp.bfloat16)
    self_weight = node_input[:feature]
    other_weight = node_input[feature:]
    node_pre = jnp.dot(normed, self_weight, preferred_element_type=jnp.float32) + jnp.dot(aggregate, other_weight, preferred_element_type=jnp.float32) + node_bias
    hidden_units = jax.nn.silu(node_pre).astype(jnp.bfloat16)
    new_latents = (latents.astype(jnp.float32) + jnp.dot(hidden_units, node_output, preferred_element_type=jnp.float32)).astype(jnp.bfloat16)
    grad_hidden = back_dot(cotangent, node_output)
    grad_node_pre = (grad_hidden * silu_slope(node_pre)).astype(jnp.bfloat16)
    grad_aggregate = back_dot(grad_node_pre, other_weight)
    grad_edge_pre = norm_back((grad_aggregate * edge_gain)[None], edge_hat, edge_inv).astype(jnp.bfloat16)
    flat_grad_pre = grad_edge_pre.reshape(edge_count * row_count, feature)
    grad_edge_in = back_dot(flat_grad_pre, edge_weight).reshape(edge_count, row_count, feature) * silu_slope(edge_in)
    grad_receive = lax.optimization_barrier(jnp.sum(grad_edge_in, axis=0)).astype(jnp.bfloat16)
    grad_normed = back_dot(grad_node_pre, self_weight) + back_dot(grad_receive, receive_weight)
    matrices = (outer_sum(flat_active, flat_grad_pre), outer_sum(normed, grad_receive), jnp.concatenate([outer_sum(normed, grad_node_pre), outer_sum(aggregate, grad_node_pre)], axis=0), outer_sum(hidden_units, cotangent))
    vectors = (lax.optimization_barrier(jnp.sum(grad_edge_in, axis=(0, 1))), lax.optimization_barrier(jnp.sum(grad_aggregate[None] * edge_hat, axis=(0, 1))), lax.optimization_barrier(jnp.sum(grad_node_pre.astype(jnp.float32), axis=0)))
    return (new_latents, grad_normed, grad_edge_in, matrices, vectors)

def reference(latents, near_index, coarse_slot, coarse_send, norm_gain, send_weight, receive_weight, edge_bias, edge_weight, edge_gain, node_input, node_bias, node_output, cotangent):
    device_count = N_LAT * N_LON
    latent_hat, latent_inv = norm_rows(latents.astype(jnp.float32))
    normed = (latent_hat * norm_gain).astype(jnp.bfloat16)
    sent = jnp.dot(normed, send_weight, preferred_element_type=jnp.float32).astype(jnp.bfloat16)
    receive_part = jnp.dot(normed, receive_weight, preferred_element_type=jnp.float32) + edge_bias
    grid = sent.reshape(N_LAT, N_LON, ROWS_DEV, D)
    western = jnp.roll(grid, 1, axis=1)[:, :, ROWS_DEV - RIM:]
    eastern = jnp.roll(grid, -1, axis=1)[:, :, :RIM]
    extended = jnp.concatenate([western, grid, eastern], axis=2).reshape(device_count, ROWS_DEV + 2 * RIM, D)
    owner = (jnp.arange(NODES) // ROWS_DEV).astype(jnp.int32)
    source = (coarse_slot // PAIR_CAP).astype(jnp.int32)
    position = (coarse_slot % PAIR_CAP).astype(jnp.int32)
    send_row = coarse_send[source, owner[None, :] * PAIR_CAP + position]
    coarse_row = (source * ROWS_DEV + send_row).astype(jnp.int32)
    near_split = jnp.transpose(near_index.reshape(DEG, device_count, ROWS_DEV), (1, 0, 2))
    coarse_split = jnp.transpose(coarse_row.reshape(CDEG, device_count, ROWS_DEV), (1, 0, 2))

    def visit(carry, pieces):
        grad_sent, matrices, vectors = carry
        own_latents, own_normed, own_receive, own_extended, own_near, own_coarse, own_cotangent = pieces
        senders = jnp.concatenate([own_extended[own_near], sent[own_coarse]], axis=0)
        new_rows, grad_normed, grad_edge_in, own_matrices, own_vectors = edge_node_pass(own_latents, own_normed, own_receive, senders, receive_weight, edge_weight, edge_gain, node_input, node_bias, node_output, own_cotangent)
        grad_sent = grad_sent.at[own_coarse.reshape(-1)].add(grad_edge_in[DEG:].reshape(-1, D))
        grad_extended = jnp.zeros((ROWS_DEV + 2 * RIM, D), jnp.float32).at[own_near.reshape(-1)].add(grad_edge_in[:DEG].reshape(-1, D))
        matrices = jax.tree.map(jnp.add, matrices, own_matrices)
        vectors = jax.tree.map(jnp.add, vectors, own_vectors)
        return ((grad_sent, matrices, vectors), (new_rows, grad_normed, grad_extended))
    start = (jnp.zeros((NODES, D), jnp.float32), (jnp.zeros((D, D), jnp.float32), jnp.zeros((D, D), jnp.float32), jnp.zeros((2 * D, D), jnp.float32), jnp.zeros((D, D), jnp.float32)), (jnp.zeros((D,), jnp.float32), jnp.zeros((D,), jnp.float32), jnp.zeros((D,), jnp.float32)))
    pieces = (latents.reshape(device_count, ROWS_DEV, D), normed.reshape(device_count, ROWS_DEV, D), receive_part.reshape(device_count, ROWS_DEV, D), extended, near_split, coarse_split, cotangent.reshape(device_count, ROWS_DEV, D))
    (grad_sent, matrices, vectors), (new_rows, grad_normed, grad_extended) = lax.scan(visit, start, pieces)
    own_part = grad_extended[:, RIM:RIM + ROWS_DEV].reshape(N_LAT, N_LON, ROWS_DEV, D)
    west_part = grad_extended[:, :RIM].reshape(N_LAT, N_LON, RIM, D)
    east_part = grad_extended[:, RIM + ROWS_DEV:].reshape(N_LAT, N_LON, RIM, D)
    own_part = own_part.at[:, :, ROWS_DEV - RIM:].add(jnp.roll(west_part, -1, axis=1))
    own_part = own_part.at[:, :, :RIM].add(jnp.roll(east_part, 1, axis=1))
    grad_sent = (grad_sent + own_part.reshape(NODES, D)).astype(jnp.bfloat16)
    grad_normed = grad_normed.reshape(NODES, D) + back_dot(grad_sent, send_weight)
    grad_latents = (cotangent.astype(jnp.float32) + norm_back(grad_normed * norm_gain, latent_hat, latent_inv)).astype(jnp.bfloat16)
    scale = float(NODES) ** (-0.5)
    grad_send = outer_sum(normed, grad_sent) * scale
    grad_vectors = jnp.stack([lax.optimization_barrier(jnp.sum(grad_normed * latent_hat, axis=0)), vectors[0], vectors[1], vectors[2]]) * scale
    return (new_rows.reshape(NODES, D), grad_latents, grad_send, matrices[1] * scale, matrices[0] * scale, matrices[2] * scale, matrices[3] * scale, grad_vectors)
```

```python
import types

import jax
import jax.numpy as jnp
from jax import lax
from jax.experimental import pallas as pl
from jax.experimental.pallas import tpu as pltpu
from jax.sharding import PartitionSpec as P

MESH = pl.DeviceIdType.MESH
EPS = 1e-05
D = 512
ROWS = 256
RIM = 128
DEG = 4
CDEG = 2
EDGES = DEG + CDEG
DEVICES = 128
CAP = 8
SLOTS = DEVICES * CAP
F32 = jnp.float32
BF16 = jnp.bfloat16

NODE_OUT, NODE_SELF, NODE_AGG, RECEIVE, EDGE, SEND = range(6)


def mm(a, b):
    return jnp.dot(a, b, preferred_element_type=F32)


def mm_bt(a, b):
    return lax.dot_general(a, b, (((1,), (1,)), ((), ())), preferred_element_type=F32)


def mm_at(a, b):
    return lax.dot_general(a, b, (((0,), (0,)), ((), ())), preferred_element_type=F32)


def mean_row(v):
    return jnp.mean(v, axis=-1, keepdims=True)


def silu_parts(v):
    gate = 0.5 * jnp.tanh(0.5 * v) + 0.5
    out = v * gate
    return out, gate + out * (1.0 - gate)


def norm_rows(v):
    centred = v - mean_row(v)
    inverse = lax.rsqrt(mean_row(centred * centred) + EPS)
    return centred * inverse, inverse


def col_sum(v):
    return jnp.sum(v, axis=0, keepdims=True)


def lane_hot(column, width):
    lanes = lax.broadcasted_iota(jnp.int32, (column.shape[0], width), 1)
    return jnp.where(lanes == column, 1.0, 0.0).astype(BF16)


def sub_hot(row, height):
    subs = lax.broadcasted_iota(jnp.int32, (height, row.shape[1]), 0)
    return jnp.where(subs == row, 1.0, 0.0).astype(BF16)


def to_pairs(rows):
    k = rows.shape[0] // CAP
    left = rows[:, : D // 2].reshape(k, CAP, D // 2)
    right = rows[:, D // 2 :].reshape(k, CAP, D // 2)
    return jnp.concatenate([left, right], axis=1).astype(BF16)


def from_pairs(pairs):
    k = pairs.shape[0]
    wide = pairs.astype(F32)
    left = wide[:, :CAP].reshape(k * CAP, D // 2)
    right = wide[:, CAP:].reshape(k * CAP, D // 2)
    return jnp.concatenate([left, right], axis=1).astype(BF16)


INPUTS = ["lat", "near", "slot", "csend", "ngain", "sw", "rw", "ebias", "ew", "egain", "ni", "nbias", "no", "cot"]
OUTPUTS = ["newlat", "glat", "res", "vout"]


def scratch():
    dma = pltpu.SemaphoreType.DMA
    half = (DEVICES, 2 * CAP, D // 2)
    return {
        "ext_n": pltpu.VMEM((ROWS + 2 * RIM, D), BF16),
        "lhat": pltpu.VMEM((ROWS, D), F32),
        "linv": pltpu.VMEM((ROWS, 1), F32),
        "pk": pltpu.VMEM(half, BF16),
        "arr": pltpu.VMEM(half, BF16),
        "pk2": pltpu.VMEM(half, BF16),
        "arr2": pltpu.VMEM(half, BF16),
        "arr_n": pltpu.VMEM((SLOTS, D), BF16),
        "cols": pltpu.VMEM((EDGES, ROWS, 1), jnp.int32),
        "recv": pltpu.VMEM((ROWS, D), F32),
        "gh": pltpu.VMEM((ROWS, D), F32),
        "npre": pltpu.VMEM((ROWS, D), F32),
        "sent_ext": pltpu.VMEM((ROWS + 2 * RIM, D), BF16),
        "act": pltpu.VMEM((EDGES, ROWS, D), BF16),
        "slope": pltpu.VMEM((EDGES, ROWS, D), F32),
        "hat": pltpu.VMEM((EDGES, ROWS, D), F32),
        "einv": pltpu.VMEM((EDGES, ROWS, 1), F32),
        "hsum": pltpu.VMEM((ROWS, D), F32),
        "cn": pltpu.VMEM((CDEG, ROWS, D), BF16),
        "geb": pltpu.VMEM((EDGES, ROWS, D), BF16),
        "gext": pltpu.VMEM((ROWS + 2 * RIM, D), F32),
        "rims": pltpu.VMEM((4, RIM, D), BF16),
        "gnp": pltpu.VMEM((ROWS, D), BF16),
        "aggr": pltpu.VMEM((ROWS, D), BF16),
        "grecv": pltpu.VMEM((ROWS, D), BF16),
        "gnb": pltpu.VMEM((ROWS, D), F32),
        "acc": pltpu.VMEM((D, D), F32),
        "part": pltpu.VMEM((6, D, D), BF16),
        "crecv": pltpu.VMEM((3, D, D), BF16),
        "s1": pltpu.VMEM((3, D, D), BF16),
        "r1": pltpu.VMEM((3, 3, D // 4, D), BF16),
        "s2": pltpu.VMEM((3, D // 4, D), BF16),
        "r2": pltpu.VMEM((3, 3, D // 16, D), BF16),
        "s3": pltpu.VMEM((3, D // 16, D), BF16),
        "r3": pltpu.VMEM((3, 3, D // 16, D // 4), BF16),
        "vec": pltpu.VMEM((4, 8, D), F32),
        "vrecv": pltpu.VMEM((4, 4, 8, D), F32),
        "hs": dma((2,)), "hr": dma((2,)), "hs2": dma((2,)), "hr2": dma((2,)),
        "as_": dma, "ar": dma, "as2": dma, "ar2": dma,
        "cs": dma((3,)), "cr": dma((3,)), "gcs": dma((3,)), "gcr": dma((3,)),
        "s1s": dma((3, 3)), "s1r": dma((3, 3)), "s2s": dma((3, 3)), "s2r": dma((3, 3)),
        "s3s": dma((3, 3)), "s3r": dma((3, 3)), "g1s": dma((3, 3)), "g1r": dma((3, 3)),
        "g2s": dma((3, 3)), "g2r": dma((3, 3)), "g3s": dma((3, 3)), "g3r": dma((3, 3)),
        "vs": dma((4, 3)), "vr": dma((4, 3)),
    }


def body(*refs):
    r = types.SimpleNamespace(**dict(zip(INPUTS + OUTPUTS + list(scratch()), refs)))
    la = lax.axis_index("lat")
    lo = lax.axis_index("lon")
    me = la * 32 + lo
    z, y, x, c = la, lo // 8, lax.rem(lo // 2, 4), lax.rem(lo, 2)

    def dev(t):
        return (t // 32, lax.rem(t, 32))

    def at(z, y, x, c):
        return (z, y * 8 + x * 2 + c)

    coord = {"x": x, "y": y, "z": z}

    def peer(axis, d):
        p = dict(coord)
        p[axis] = lax.rem(coord[axis] + d, 4)
        return at(p["z"], p["y"], p["x"], c), p[axis]

    def rcopy(src, dst, ssem, rsem, device):
        return pltpu.make_async_remote_copy(src, dst, ssem, rsem, device_id=device, device_id_type=MESH)

    bar = pltpu.get_barrier_semaphore()

    @pl.loop(1, DEVICES)
    def _(k):
        pl.semaphore_signal(bar, inc=1, device_id=dev(lax.rem(me + k, DEVICES)), device_id_type=MESH)

    h, inv = norm_rows(r.lat[...].astype(F32))
    r.lhat[...] = h
    r.linv[...] = inv
    r.ext_n[RIM : RIM + ROWS] = (h * r.ngain[...]).astype(BF16)

    idx = jnp.concatenate([r.near[...], r.slot[...], jnp.zeros((2, ROWS), jnp.int32)], axis=0)
    idx_t = jnp.transpose(idx)
    for k in range(EDGES):
        r.cols[k] = idx_t[:, k : k + 1]
    send_t = jnp.transpose(r.csend[...].reshape(8, 128))
    for j in range(8):
        rows = mm(lane_hot(send_t[:, j : j + 1], ROWS), r.ext_n[RIM : RIM + ROWS])
        r.pk[16 * j : 16 * j + 16] = to_pairs(rows)

    pl.semaphore_wait(bar, DEVICES - 1)

    west = (la, lax.rem(lo + 31, 32))
    east = (la, lax.rem(lo + 1, 32))
    halo = [
        rcopy(r.ext_n.at[pl.ds(2 * RIM, RIM)], r.ext_n.at[pl.ds(0, RIM)], r.hs.at[0], r.hr.at[0], east),
        rcopy(r.ext_n.at[pl.ds(RIM, RIM)], r.ext_n.at[pl.ds(3 * RIM, RIM)], r.hs.at[1], r.hr.at[1], west),
    ]
    for q in halo:
        q.start()

    @pl.loop(1, DEVICES)
    def _(k):
        t = lax.rem(me + k, DEVICES)
        rcopy(r.pk.at[t], r.arr.at[me], r.as_, r.ar, dev(t)).start()

    r.arr[me] = r.pk[me]

    def own():
        return r.ext_n[RIM : RIM + ROWS]

    r.recv[...] = mm(own(), r.rw[...]) + r.ebias[...]
    r.sent_ext[RIM : RIM + ROWS] = mm(own(), r.sw[...]).astype(BF16)
    r.gh[...] = mm_bt(r.cot[...], r.no[...])
    r.npre[...] = mm(own(), r.ni[0:D]) + r.nbias[...]
    r.hsum[...] = jnp.zeros((ROWS, D), F32)
    for q in halo:
        q.wait()
    r.sent_ext[0:RIM] = mm(r.ext_n[0:RIM], r.sw[...]).astype(BF16)
    r.sent_ext[3 * RIM : 4 * RIM] = mm(r.ext_n[3 * RIM : 4 * RIM], r.sw[...]).astype(BF16)

    def edge_forward(k, senders):
        a, s = silu_parts(senders + r.recv[...])
        a = a.astype(BF16)
        r.act[k] = a
        r.slope[k] = s
        h, inv = norm_rows(mm(a, r.ew[...]))
        r.hat[k] = h
        r.einv[k] = inv
        r.hsum[...] += h

    @pl.loop(0, DEG)
    def _(k):
        edge_forward(k, mm(lane_hot(r.cols[k], ROWS + 2 * RIM), r.sent_ext[...]))

    everything = rcopy(r.pk.at[pl.ds(0, DEVICES - 1)], r.arr.at[pl.ds(0, DEVICES - 1)], r.as_, r.ar, west)
    everything.wait()

    @pl.loop(0, 8)
    def _(j):
        r.arr_n[pl.ds(pl.multiple_of(j * 128, 128), 128)] = from_pairs(r.arr[pl.ds(j * 16, 16)])

    @pl.loop(0, CDEG)
    def _(k):
        rows = mm(lane_hot(r.cols[DEG + k], SLOTS), r.arr_n[...]).astype(BF16)
        r.cn[k] = rows
        edge_forward(DEG + k, mm(rows, r.sw[...]).astype(BF16).astype(F32))

    aggregate = (r.hsum[...] * r.egain[...]).astype(BF16)
    hidden, node_slope = silu_parts(r.npre[...] + mm(aggregate, r.ni[D : 2 * D]))
    hidden = hidden.astype(BF16)
    r.newlat[...] = (r.lat[...].astype(F32) + mm(hidden, r.no[...])).astype(BF16)
    gnp = (r.gh[...] * node_slope).astype(BF16)
    r.gnp[...] = gnp
    r.aggr[...] = aggregate
    gagg = mm_bt(gnp, r.ni[D : 2 * D])
    r.vec[0] = jnp.zeros((8, D), F32)
    r.vec[0, 2:3] = col_sum(gagg * r.hsum[...])
    r.vec[0, 3:4] = col_sum(gnp.astype(F32))
    r.part[NODE_OUT] = mm_at(hidden, r.cot[...]).astype(BF16)
    r.part[NODE_SELF] = mm_at(own(), r.gnp[...]).astype(BF16)

    def core_copy(p):
        return rcopy(r.part.at[2 * p + 1 - c], r.crecv.at[p], r.cs.at[p], r.cr.at[p], at(z, y, x, 1 - c))

    core_copy(0).start()
    r.part[NODE_AGG] = mm_at(r.aggr[...], r.gnp[...]).astype(BF16)

    up = gagg * r.egain[...]
    r.npre[...] = up - mean_row(up)
    r.gh[...] = up
    r.recv[...] = jnp.zeros((ROWS, D), F32)
    r.acc[...] = jnp.zeros((D, D), F32)

    def edge_backward(k):
        h = r.hat[k]
        g = (r.einv[k] * (r.npre[...] - h * mean_row(r.gh[...] * h))).astype(BF16)
        ge = mm_bt(g, r.ew[...]) * r.slope[k]
        r.recv[...] += ge
        r.geb[k] = ge.astype(BF16)
        r.acc[...] += mm_at(r.act[k], g)

    pl.loop(DEG, EDGES)(edge_backward)

    for j in range(4):
        block = jnp.zeros((256, D), F32)
        for k in range(CDEG):
            block += mm(sub_hot(r.slot[k : k + 1, :] - 256 * j, 256), r.geb[DEG + k])
        r.pk2[32 * j : 32 * j + 32] = to_pairs(block)

    @pl.loop(1, DEVICES)
    def _(k):
        t = lax.rem(me + k, DEVICES)
        rcopy(r.pk2.at[t], r.arr2.at[me], r.as2, r.ar2, dev(t)).start()

    r.arr2[me] = r.pk2[me]

    pl.loop(0, DEG)(edge_backward)
    r.part[EDGE] = r.acc[...].astype(BF16)
    for j in range(4):
        block = jnp.zeros((RIM, D), F32)
        for k in range(DEG):
            block += mm(sub_hot(r.near[k : k + 1, :] - RIM * j, RIM), r.geb[k])
        r.gext[RIM * j : RIM * j + RIM] = block
    r.rims[0] = r.gext[0:RIM].astype(BF16)
    r.rims[1] = r.gext[3 * RIM : 4 * RIM].astype(BF16)
    halo_back = [
        rcopy(r.rims.at[1], r.rims.at[2], r.hs2.at[0], r.hr2.at[0], east),
        rcopy(r.rims.at[0], r.rims.at[3], r.hs2.at[1], r.hr2.at[1], west),
    ]
    for q in halo_back:
        q.start()
    r.vec[0, 1:2] = col_sum(r.recv[...])
    r.grecv[...] = r.recv[...].astype(BF16)
    r.part[RECEIVE] = mm_at(own(), r.grecv[...]).astype(BF16)
    r.acc[...] = mm_at(r.ext_n[...], r.gext[...].astype(BF16))
    for k in range(CDEG):
        r.acc[...] += mm_at(r.cn[k], r.geb[DEG + k])
    r.part[SEND] = r.acc[...].astype(BF16)
    core_copy(1).start()
    core_copy(2).start()
    local_back = mm_bt(r.gnp[...], r.ni[0:D]) + mm_bt(r.grecv[...], r.rw[...])
    r.gnb[...] = local_back
    through_sent = jnp.sum(r.sw[...].astype(F32) * r.acc[...], axis=1, keepdims=True)
    through_sent = jnp.transpose(jnp.broadcast_to(through_sent, (D, 128)))[0:1]
    r.vec[0, 0:1] = col_sum(r.lhat[...] * local_back) + through_sent / r.ngain[...]

    orders = ("xyz", "yzx", "zxy")
    scale = float(ROWS * DEVICES) ** -0.5

    def rs1(p, d):
        device, pos = peer(orders[p][0], d)
        return rcopy(r.s1.at[p, pl.ds(pl.multiple_of(pos * 128, 128), 128)], r.r1.at[p, d - 1], r.s1s.at[p, d - 1], r.s1r.at[p, d - 1], device)

    def rs2(p, d):
        device, pos = peer(orders[p][1], d)
        return rcopy(r.s2.at[p, pl.ds(pl.multiple_of(pos * 32, 32), 32)], r.r2.at[p, d - 1], r.s2s.at[p, d - 1], r.s2r.at[p, d - 1], device)

    def rs3(p, d):
        device, pos = peer(orders[p][2], d)
        return rcopy(r.s3.at[p, :, pl.ds(pl.multiple_of(pos * 128, 128), 128)], r.r3.at[p, d - 1], r.s3s.at[p, d - 1], r.s3r.at[p, d - 1], device)

    def spot(p, level):
        a, b, e = (coord[axis] for axis in orders[p])
        rows, lanes = a * 128 + b * 32, pl.ds(pl.multiple_of(e * 128, 128), 128)
        if level == 3:
            return r.res.at[2 * p + c, pl.ds(pl.multiple_of(rows, 32), 32), lanes]
        if level == 2:
            return r.res.at[2 * p + c, pl.ds(pl.multiple_of(rows, 32), 32)]
        if level == 1:
            return r.res.at[2 * p + c, pl.ds(pl.multiple_of(a * 128, 128), 128)]
        return r.res.at[2 * p + c]

    def ag(p, level, d):
        ssem, rsem = {3: (r.g3s, r.g3r), 2: (r.g2s, r.g2r), 1: (r.g1s, r.g1r)}[level]
        device, _ = peer(orders[p][level - 1], d)
        return rcopy(spot(p, level), spot(p, level), ssem.at[p, d - 1], rsem.at[p, d - 1], device)

    def ag_core(p):
        return rcopy(spot(p, 0), spot(p, 0), r.gcs.at[p], r.gcr.at[p], at(z, y, x, 1 - c))

    def vec_core():
        return rcopy(r.vec.at[0], r.vrecv.at[0, 1], r.vs.at[0, 0], r.vr.at[0, 0], at(z, y, x, 1 - c))

    def vec_ring(level, d):
        axis = "xyz"[level - 1]
        device, _ = peer(axis, d)
        return rcopy(r.vec.at[level], r.vrecv.at[level, d], r.vs.at[level, d - 1], r.vr.at[level, d - 1], device)

    def vec_sum(level):
        axis = "xyz"[level - 1]
        mine = coord[axis]
        r.vrecv[level, 0] = r.vec[level]
        total = jnp.zeros((8, D), F32)
        for i in range(4):
            total += r.vrecv[level, lax.rem(mine - i + 4, 4)]
        return total

    def vec_total(level):
        if level == 0:
            return r.vec[0] + r.vrecv[0, 1]
        return vec_sum(level)

    vec_core().start()

    def fold_core(p):
        core_copy(p).wait()

        @pl.loop(0, 4)
        def _(j):
            rows = pl.ds(pl.multiple_of(j * 128, 128), 128)
            r.s1[p, rows] = (r.part[2 * p + c, rows].astype(F32) + r.crecv[p, rows].astype(F32)).astype(BF16)

        for d in (2, 1, 3):
            rs1(p, d).start()

    def fold1(p):
        total = r.s1[p, pl.ds(pl.multiple_of(coord[orders[p][0]] * 128, 128), 128)].astype(F32)
        for d in (1, 3, 2):
            rs1(p, d).wait()
            total += r.r1[p, d - 1].astype(F32)
        r.s2[p] = total.astype(BF16)
        for d in (2, 1, 3):
            rs2(p, d).start()

    def fold2(p):
        total = r.s2[p, pl.ds(pl.multiple_of(coord[orders[p][1]] * 32, 32), 32)].astype(F32)
        for d in (1, 3, 2):
            rs2(p, d).wait()
            total += r.r2[p, d - 1].astype(F32)
        r.s3[p] = total.astype(BF16)
        for d in (2, 1, 3):
            rs3(p, d).start()

    def fold3(p):
        total = r.s3[p, :, pl.ds(pl.multiple_of(coord[orders[p][2]] * 128, 128), 128)].astype(F32)
        for d in (1, 3, 2):
            rs3(p, d).wait()
            total += r.r3[p, d - 1].astype(F32)
        spot(p, 3)[...] = (total * scale).astype(BF16)
        for d in (2, 1, 3):
            ag(p, 3, d).start()

    def spread(p, level):
        for d in (1, 3, 2):
            ag(p, level, d).wait()
        if level > 1:
            for d in (2, 1, 3):
                ag(p, level - 1, d).start()
        else:
            ag_core(p).start()

    def vec_step(level):
        if level == 0:
            vec_core().wait()
        else:
            for d in (1, 2, 3):
                vec_ring(level, d).wait()
        total = vec_total(level)
        if level < 3:
            r.vec[level + 1] = total
            for d in (1, 2, 3):
                vec_ring(level + 1, d).start()
        else:
            r.vout[...] = total[0:4] * scale

    for p in range(3):
        fold_core(p)
    vec_step(0)
    for p in range(3):
        fold1(p)
    vec_step(1)
    for p in range(3):
        fold2(p)
    vec_step(2)
    for p in range(3):
        fold3(p)
    vec_step(3)

    for q in halo_back:
        q.wait()
    grad_sent = r.gext[RIM : RIM + ROWS] + r.rims[2:4].reshape(ROWS, D).astype(F32)
    rcopy(r.pk2.at[pl.ds(0, DEVICES - 1)], r.arr2.at[pl.ds(0, DEVICES - 1)], r.as2, r.ar2, west).wait()

    @pl.loop(0, 8)
    def _(j):
        r.arr_n[pl.ds(pl.multiple_of(j * 128, 128), 128)] = from_pairs(r.arr2[pl.ds(j * 16, 16)])

    grad_sent += mm(sub_hot(r.csend[...], ROWS), r.arr_n[...])
    up = (r.gnb[...] + mm_bt(grad_sent.astype(BF16), r.sw[...])) * r.ngain[...]
    h = r.lhat[...]
    back = r.linv[...] * (up - mean_row(up) - h * mean_row(up * h))
    r.glat[...] = (r.cot[...].astype(F32) + back).astype(BF16)

    for level in (3, 2, 1):
        for p in range(3):
            spread(p, level)
    for p in range(3):
        ag_core(p).wait()


def per_device(
    latents, near_index, coarse_slot, coarse_send, norm_gain, send_weight, receive_weight, edge_bias,
    edge_weight, edge_gain, node_input, node_bias, node_output, cotangent,
):
    whole = pl.BlockSpec(memory_space=pltpu.VMEM)
    new_latents, grad_latents, sums, vectors = pl.pallas_call(
        body,
        out_shape=(
            jax.ShapeDtypeStruct((ROWS, D), BF16),
            jax.ShapeDtypeStruct((ROWS, D), BF16),
            jax.ShapeDtypeStruct((6, D, D), BF16),
            jax.ShapeDtypeStruct((4, D), F32),
        ),
        in_specs=[whole] * 14,
        out_specs=(whole,) * 4,
        scratch_shapes=list(scratch().values()),
        compiler_params=pltpu.CompilerParams(
            collective_id=0, has_side_effects=True, vmem_limit_bytes=58 * 2**20
        ),
    )(
        latents, near_index, coarse_slot, coarse_send, norm_gain.reshape(1, D), send_weight, receive_weight,
        edge_bias.reshape(1, D), edge_weight, edge_gain.reshape(1, D), node_input, node_bias.reshape(1, D),
        node_output, cotangent,
    )
    wide = sums.astype(F32)
    return (
        new_latents, grad_latents, wide[SEND], wide[RECEIVE], wide[EDGE],
        wide[NODE_SELF : NODE_AGG + 1].reshape(2 * D, D), wide[NODE_OUT], vectors,
    )


def solution(mesh):
    rows, whole = P(("lat", "lon"), None), P()
    split = P(None, ("lat", "lon"))
    return jax.shard_map(
        per_device,
        mesh=mesh,
        in_specs=(rows, split, split, rows) + (whole,) * 9 + (rows,),
        out_specs=(rows, rows) + (whole,) * 6,
        check_vma=False,
    )
```

```python
import types

import jax
import jax.numpy as jnp
from jax import lax
from jax.experimental import pallas as pl
from jax.experimental.pallas import tpu as pltpu
from jax.sharding import PartitionSpec as P

MESH = pl.DeviceIdType.MESH
EPS = 1e-05
D = 512
ROWS = 256
RIM = 128
DEG = 4
CDEG = 2
EDGES = DEG + CDEG
DEVICES = 128
CAP = 8
SLOTS = DEVICES * CAP
F32 = jnp.float32
BF16 = jnp.bfloat16

NODE_OUT, NODE_SELF, NODE_AGG, RECEIVE, EDGE, SEND = range(6)


def exchange_order():
    cube = [(i, j, k) for i in range(4) for j in range(4) for k in range(4)]
    cube.sort(key=lambda d: (-sum(min(v, 4 - v) for v in d), [-v for v in d]))
    order = []
    for d in cube:
        for sign in (1, -1):
            for turn in range(3):
                e = tuple((sign * v) % 4 for v in d[turn:] + d[:turn])
                if e not in order:
                    order.append(e)
    return [e + (core,) for e in order for core in (0, 1) if any(e) or core]


ORDER = exchange_order()


def mm(a, b):
    return jnp.dot(a, b, preferred_element_type=F32)


def mm_bt(a, b):
    return lax.dot_general(a, b, (((1,), (1,)), ((), ())), preferred_element_type=F32)


def mm_at(a, b):
    return lax.dot_general(a, b, (((0,), (0,)), ((), ())), preferred_element_type=F32)


def mean_row(v):
    return jnp.mean(v, axis=-1, keepdims=True)


def silu_parts(v):
    gate = 0.5 * jnp.tanh(0.5 * v) + 0.5
    out = v * gate
    return out, gate + out * (1.0 - gate)


def norm_rows(v):
    centred = v - mean_row(v)
    inverse = lax.rsqrt(mean_row(centred * centred) + EPS)
    return centred * inverse, inverse


def col_sum(v):
    return jnp.sum(v, axis=0, keepdims=True)


def lane_hot(column, width):
    lanes = lax.broadcasted_iota(jnp.int32, (column.shape[0], width), 1)
    return jnp.where(lanes == column, 1.0, 0.0).astype(BF16)


def sub_hot(row, height):
    subs = lax.broadcasted_iota(jnp.int32, (height, row.shape[1]), 0)
    return jnp.where(subs == row, 1.0, 0.0).astype(BF16)


def to_pairs(rows):
    k = rows.shape[0] // CAP
    left = rows[:, : D // 2].reshape(k, CAP, D // 2)
    right = rows[:, D // 2 :].reshape(k, CAP, D // 2)
    return jnp.concatenate([left, right], axis=1).astype(BF16)


def from_pairs(pairs):
    k = pairs.shape[0]
    wide = pairs.astype(F32)
    left = wide[:, :CAP].reshape(k * CAP, D // 2)
    right = wide[:, CAP:].reshape(k * CAP, D // 2)
    return jnp.concatenate([left, right], axis=1).astype(BF16)


INPUTS = ["lat", "near", "slot", "csend", "ngain", "sw", "rw", "ebias", "ew", "egain", "ni", "nbias", "no", "cot"]
OUTPUTS = ["newlat", "glat", "res", "vout"]


def scratch():
    dma = pltpu.SemaphoreType.DMA
    half = (DEVICES, 2 * CAP, D // 2)
    return {
        "ext_n": pltpu.VMEM((ROWS + 2 * RIM, D), BF16),
        "lhat": pltpu.VMEM((ROWS, D), F32),
        "linv": pltpu.VMEM((ROWS, 1), F32),
        "pk": pltpu.VMEM(half, BF16),
        "arr": pltpu.VMEM(half, BF16),
        "pk2": pltpu.VMEM(half, BF16),
        "arr2": pltpu.VMEM(half, BF16),
        "arr_n": pltpu.VMEM((SLOTS, D), BF16),
        "cols": pltpu.VMEM((EDGES, ROWS, 1), jnp.int32),
        "recv": pltpu.VMEM((ROWS, D), F32),
        "gh": pltpu.VMEM((ROWS, D), F32),
        "npre": pltpu.VMEM((ROWS, D), F32),
        "sent_ext": pltpu.VMEM((ROWS + 2 * RIM, D), BF16),
        "act": pltpu.VMEM((EDGES, ROWS, D), BF16),
        "slope": pltpu.VMEM((EDGES, ROWS, D), F32),
        "hat": pltpu.VMEM((EDGES, ROWS, D), F32),
        "einv": pltpu.VMEM((EDGES, ROWS, 1), F32),
        "hsum": pltpu.VMEM((ROWS, D), F32),
        "cn": pltpu.VMEM((CDEG, ROWS, D), BF16),
        "geb": pltpu.VMEM((EDGES, ROWS, D), BF16),
        "gext": pltpu.VMEM((ROWS + 2 * RIM, D), F32),
        "rims": pltpu.VMEM((4, RIM, D), BF16),
        "gnp": pltpu.VMEM((ROWS, D), BF16),
        "aggr": pltpu.VMEM((ROWS, D), BF16),
        "grecv": pltpu.VMEM((ROWS, D), BF16),
        "gnb": pltpu.VMEM((ROWS, D), F32),
        "acc": pltpu.VMEM((D, D), F32),
        "part": pltpu.VMEM((6, D, D), BF16),
        "crecv": pltpu.VMEM((6, D // 2, D), BF16),
        "s1": pltpu.VMEM((6, D // 2, D), BF16),
        "r1": pltpu.VMEM((6, 3, D // 8, D), BF16),
        "s2": pltpu.VMEM((6, D // 8, D), BF16),
        "r2": pltpu.VMEM((6, 3, D // 32, D), BF16),
        "r3": pltpu.VMEM((6, 4, D // 32, D), BF16),
        "vec": pltpu.VMEM((4, 8, D), F32),
        "vrecv": pltpu.VMEM((4, 4, 8, D), F32),
        "hs": dma((2,)), "hr": dma((2,)), "hs2": dma((2,)), "hr2": dma((2,)),
        "as_": dma, "ar": dma, "as2": dma, "ar2": dma,
        "cs": dma((6,)), "cr": dma((6,)), "gcs": dma((6,)), "gcr": dma((6,)),
        "s1s": dma((6, 3)), "s1r": dma((6, 3)), "s2s": dma((6, 3)), "s2r": dma((6, 3)),
        "s3s": dma((6, 3)), "s3r": dma((6, 3)), "g1s": dma((6, 3)), "g1r": dma((6, 3)),
        "g2s": dma((6, 3)), "g2r": dma((6, 3)),
        "vs": dma((4, 3)), "vr": dma((4, 3)),
    }


def body(*refs):
    r = types.SimpleNamespace(**dict(zip(INPUTS + OUTPUTS + list(scratch()), refs)))
    la = lax.axis_index("lat")
    lo = lax.axis_index("lon")
    me = la * 32 + lo
    z, y, x, c = la, lo // 8, lax.rem(lo // 2, 4), lax.rem(lo, 2)

    def at(z, y, x, c):
        return (z, y * 8 + x * 2 + c)

    coord = {"x": x, "y": y, "z": z}

    def peer(axis, d):
        p = dict(coord)
        p[axis] = lax.rem(coord[axis] + d, 4)
        return at(p["z"], p["y"], p["x"], c), p[axis]

    def rcopy(src, dst, ssem, rsem, device):
        return pltpu.make_async_remote_copy(src, dst, ssem, rsem, device_id=device, device_id_type=MESH)

    orders = {m: ("xyz", "yzx", "zxy")[m % 3] for m in range(6)}
    scale = float(ROWS * DEVICES) ** -0.5
    other = at(z, y, x, 1 - c)

    def half(core):
        return pl.ds(pl.multiple_of(core * 256, 256), 256)

    def core_copy(m):
        return rcopy(r.part.at[m, half(1 - c)], r.crecv.at[m], r.cs.at[m], r.cr.at[m], other)

    def rs1(m, d):
        device, pos = peer(orders[m][0], d)
        rows = pl.ds(pl.multiple_of(pos * 64, 64), 64)
        return rcopy(r.s1.at[m, rows], r.r1.at[m, d - 1], r.s1s.at[m, d - 1], r.s1r.at[m, d - 1], device)

    def rs2(m, d):
        device, pos = peer(orders[m][1], d)
        rows = pl.ds(pl.multiple_of(pos * 16, 16), 16)
        return rcopy(r.s2.at[m, rows], r.r2.at[m, d - 1], r.s2s.at[m, d - 1], r.s2r.at[m, d - 1], device)

    def swap3(m, d):
        device, _ = peer(orders[m][2], d)
        return rcopy(r.r3.at[m, 0], r.r3.at[m, d], r.s3s.at[m, d - 1], r.s3r.at[m, d - 1], device)

    def spot(m, level):
        a, b = coord[orders[m][0]] * 64, coord[orders[m][1]] * 16
        if level == 2:
            return r.res.at[m, pl.ds(pl.multiple_of(c * 256 + a + b, 16), 16)]
        if level == 1:
            return r.res.at[m, pl.ds(pl.multiple_of(c * 256 + a, 64), 64)]
        return r.res.at[m, half(c)]

    def ag(m, level, d):
        ssem, rsem = {2: (r.g2s, r.g2r), 1: (r.g1s, r.g1r)}[level]
        device, _ = peer(orders[m][level - 1], d)
        return rcopy(spot(m, level), spot(m, level), ssem.at[m, d - 1], rsem.at[m, d - 1], device)

    def ag_core(m):
        return rcopy(spot(m, 0), spot(m, 0), r.gcs.at[m], r.gcr.at[m], other)

    def fold_core(m):
        core_copy(m).wait()
        r.s1[m] = (r.part[m, half(c)].astype(F32) + r.crecv[m].astype(F32)).astype(BF16)
        for d in (2, 1, 3):
            rs1(m, d).start()

    def fold1(m):
        total = r.s1[m, pl.ds(pl.multiple_of(coord[orders[m][0]] * 64, 64), 64)].astype(F32)
        for d in (1, 3, 2):
            rs1(m, d).wait()
            total += r.r1[m, d - 1].astype(F32)
        r.s2[m] = total.astype(BF16)
        for d in (2, 1, 3):
            rs2(m, d).start()

    def fold2(m):
        total = r.s2[m, pl.ds(pl.multiple_of(coord[orders[m][1]] * 16, 16), 16)].astype(F32)
        for d in (1, 3, 2):
            rs2(m, d).wait()
            total += r.r2[m, d - 1].astype(F32)
        r.r3[m, 0] = total.astype(BF16)
        for d in (2, 1, 3):
            swap3(m, d).start()

    def fold3(m):
        for d in (1, 3, 2):
            swap3(m, d).wait()
        total = jnp.zeros((16, D), F32)
        for i in range(4):
            total += r.r3[m, lax.rem(coord[orders[m][2]] - i + 4, 4)].astype(F32)
        spot(m, 2)[...] = (total * scale).astype(BF16)
        for d in (2, 1, 3):
            ag(m, 2, d).start()

    def spread(m, level):
        for d in (1, 3, 2):
            ag(m, level, d).wait()
        if level == 2:
            for d in (2, 1, 3):
                ag(m, 1, d).start()
        else:
            ag_core(m).start()

    def vec_copies(level):
        if level == 0:
            return [rcopy(r.vec.at[0], r.vrecv.at[0, 1], r.vs.at[0, 0], r.vr.at[0, 0], other)]
        return [
            rcopy(r.vec.at[level], r.vrecv.at[level, d], r.vs.at[level, d - 1], r.vr.at[level, d - 1], peer("xyz"[level - 1], d)[0])
            for d in (1, 2, 3)
        ]

    def vec_step(level):
        for q in vec_copies(level):
            q.wait()
        if level == 0:
            total = r.vec[0] + r.vrecv[0, 1]
        else:
            r.vrecv[level, 0] = r.vec[level]
            total = jnp.zeros((8, D), F32)
            for i in range(4):
                total += r.vrecv[level, lax.rem(coord["xyz"[level - 1]] - i + 4, 4)]
        if level < 3:
            r.vec[level + 1] = total
            for q in vec_copies(level + 1):
                q.start()
        else:
            r.vout[...] = total[0:4] * scale

    bar = pltpu.get_barrier_semaphore()

    zs = [lax.rem(z + i, 4) for i in range(4)]
    ys = [lax.rem(y + i, 4) * 8 for i in range(4)]
    xs = [lax.rem(x + i, 4) * 2 for i in range(4)]
    cores = [c, 1 - c]

    def away(d):
        return (zs[d[0]], ys[d[1]] + xs[d[2]] + cores[d[3]])

    for d in ORDER:
        pl.semaphore_signal(bar, inc=1, device_id=away(d), device_id_type=MESH)

    h, inv = norm_rows(r.lat[...].astype(F32))
    r.lhat[...] = h
    r.linv[...] = inv
    r.ext_n[RIM : RIM + ROWS] = (h * r.ngain[...]).astype(BF16)

    idx = jnp.concatenate([r.near[...], r.slot[...], jnp.zeros((2, ROWS), jnp.int32)], axis=0)
    idx_t = jnp.transpose(idx)
    for k in range(EDGES):
        r.cols[k] = idx_t[:, k : k + 1]
    send_t = jnp.transpose(r.csend[...].reshape(8, 128))
    for j in range(8):
        rows = mm(lane_hot(send_t[:, j : j + 1], ROWS), r.ext_n[RIM : RIM + ROWS])
        r.pk[16 * j : 16 * j + 16] = to_pairs(rows)

    pl.semaphore_wait(bar, DEVICES - 1)

    west = (la, lax.rem(lo + 31, 32))
    east = (la, lax.rem(lo + 1, 32))
    halo = [
        rcopy(r.ext_n.at[pl.ds(2 * RIM, RIM)], r.ext_n.at[pl.ds(0, RIM)], r.hs.at[0], r.hr.at[0], east),
        rcopy(r.ext_n.at[pl.ds(RIM, RIM)], r.ext_n.at[pl.ds(3 * RIM, RIM)], r.hs.at[1], r.hr.at[1], west),
    ]
    for q in halo:
        q.start()

    for d in ORDER:
        t = away(d)
        rcopy(r.pk.at[t[0] * 32 + t[1]], r.arr.at[me], r.as_, r.ar, t).start()

    r.arr[me] = r.pk[me]

    def own():
        return r.ext_n[RIM : RIM + ROWS]

    r.recv[...] = mm(own(), r.rw[...]) + r.ebias[...]
    r.sent_ext[RIM : RIM + ROWS] = mm(own(), r.sw[...]).astype(BF16)
    r.gh[...] = mm_bt(r.cot[...], r.no[...])
    r.npre[...] = mm(own(), r.ni[0:D]) + r.nbias[...]
    r.hsum[...] = jnp.zeros((ROWS, D), F32)
    for q in halo:
        q.wait()
    r.sent_ext[0:RIM] = mm(r.ext_n[0:RIM], r.sw[...]).astype(BF16)
    r.sent_ext[3 * RIM : 4 * RIM] = mm(r.ext_n[3 * RIM : 4 * RIM], r.sw[...]).astype(BF16)

    def edge_forward(k, senders):
        a, s = silu_parts(senders + r.recv[...])
        a = a.astype(BF16)
        r.act[k] = a
        r.slope[k] = s
        h, inv = norm_rows(mm(a, r.ew[...]))
        r.hat[k] = h
        r.einv[k] = inv
        r.hsum[...] += h

    @pl.loop(0, DEG)
    def _(k):
        edge_forward(k, mm(lane_hot(r.cols[k], ROWS + 2 * RIM), r.sent_ext[...]))

    everything = rcopy(r.pk.at[pl.ds(0, DEVICES - 1)], r.arr.at[pl.ds(0, DEVICES - 1)], r.as_, r.ar, west)
    everything.wait()

    @pl.loop(0, 8)
    def _(j):
        r.arr_n[pl.ds(pl.multiple_of(j * 128, 128), 128)] = from_pairs(r.arr[pl.ds(j * 16, 16)])

    @pl.loop(0, CDEG)
    def _(k):
        rows = mm(lane_hot(r.cols[DEG + k], SLOTS), r.arr_n[...]).astype(BF16)
        r.cn[k] = rows
        edge_forward(DEG + k, mm(rows, r.sw[...]).astype(BF16).astype(F32))

    aggregate = (r.hsum[...] * r.egain[...]).astype(BF16)
    hidden, node_slope = silu_parts(r.npre[...] + mm(aggregate, r.ni[D : 2 * D]))
    hidden = hidden.astype(BF16)
    r.newlat[...] = (r.lat[...].astype(F32) + mm(hidden, r.no[...])).astype(BF16)
    gnp = (r.gh[...] * node_slope).astype(BF16)
    r.gnp[...] = gnp
    r.aggr[...] = aggregate
    gagg = mm_bt(gnp, r.ni[D : 2 * D])
    r.vec[0] = jnp.zeros((8, D), F32)
    r.vec[0, 2:3] = col_sum(gagg * r.hsum[...])
    r.vec[0, 3:4] = col_sum(gnp.astype(F32))
    r.part[NODE_OUT] = mm_at(hidden, r.cot[...]).astype(BF16)
    r.part[NODE_SELF] = mm_at(own(), r.gnp[...]).astype(BF16)

    r.part[NODE_AGG] = mm_at(r.aggr[...], r.gnp[...]).astype(BF16)
    early, late = (NODE_OUT, NODE_SELF, NODE_AGG), (RECEIVE, EDGE, SEND)
    for m in early:
        core_copy(m).start()

    up = gagg * r.egain[...]
    r.npre[...] = up - mean_row(up)
    r.gh[...] = up
    r.recv[...] = jnp.zeros((ROWS, D), F32)
    r.acc[...] = jnp.zeros((D, D), F32)

    def edge_backward(k):
        h = r.hat[k]
        g = (r.einv[k] * (r.npre[...] - h * mean_row(r.gh[...] * h))).astype(BF16)
        ge = mm_bt(g, r.ew[...]) * r.slope[k]
        r.recv[...] += ge
        r.geb[k] = ge.astype(BF16)
        r.acc[...] += mm_at(r.act[k], g)

    pl.loop(DEG, EDGES)(edge_backward)
    for m in early:
        fold_core(m)
    pl.loop(0, DEG)(edge_backward)

    r.part[EDGE] = r.acc[...].astype(BF16)
    core_copy(EDGE).start()
    r.grecv[...] = r.recv[...].astype(BF16)
    r.part[RECEIVE] = mm_at(own(), r.grecv[...]).astype(BF16)
    core_copy(RECEIVE).start()
    for j in range(4):
        block = jnp.zeros((RIM, D), F32)
        for k in range(DEG):
            block += mm(sub_hot(r.near[k : k + 1, :] - RIM * j, RIM), r.geb[k])
        r.gext[RIM * j : RIM * j + RIM] = block
    r.acc[...] = mm_at(r.ext_n[...], r.gext[...].astype(BF16))
    for k in range(CDEG):
        r.acc[...] += mm_at(r.cn[k], r.geb[DEG + k])
    r.part[SEND] = r.acc[...].astype(BF16)
    core_copy(SEND).start()
    for m in early:
        fold1(m)
    for m in (EDGE, RECEIVE, SEND):
        fold_core(m)

    r.rims[0] = r.gext[0:RIM].astype(BF16)
    r.rims[1] = r.gext[3 * RIM : 4 * RIM].astype(BF16)
    halo_back = [
        rcopy(r.rims.at[1], r.rims.at[2], r.hs2.at[0], r.hr2.at[0], east),
        rcopy(r.rims.at[0], r.rims.at[3], r.hs2.at[1], r.hr2.at[1], west),
    ]
    for q in halo_back:
        q.start()
    for j in range(4):
        block = jnp.zeros((256, D), F32)
        for k in range(CDEG):
            block += mm(sub_hot(r.slot[k : k + 1, :] - 256 * j, 256), r.geb[DEG + k])
        r.pk2[32 * j : 32 * j + 32] = to_pairs(block)
    r.arr2[me] = r.pk2[me]

    def send_back(first, last):
        for d in ORDER[first:last]:
            t = away(d)
            rcopy(r.pk2.at[t[0] * 32 + t[1]], r.arr2.at[me], r.as2, r.ar2, t).start()

    send_back(0, 32)
    local_back = mm_bt(r.gnp[...], r.ni[0:D]) + mm_bt(r.grecv[...], r.rw[...])
    r.gnb[...] = local_back
    through_sent = jnp.sum(r.sw[...].astype(F32) * r.acc[...], axis=1, keepdims=True)
    through_sent = jnp.transpose(jnp.broadcast_to(through_sent, (D, 128)))[0:1]
    r.vec[0, 0:1] = col_sum(r.lhat[...] * local_back) + through_sent / r.ngain[...]
    r.vec[0, 1:2] = col_sum(r.recv[...])
    for q in vec_copies(0):
        q.start()

    for m in early:
        fold2(m)
    vec_step(0)
    send_back(32, 64)
    for m in late:
        fold1(m)
    for m in early:
        fold3(m)
    send_back(64, 96)
    vec_step(1)
    for m in late:
        fold2(m)
    for m in early:
        spread(m, 2)
    send_back(96, 127)
    vec_step(2)
    for m in late:
        fold3(m)
    for m in early:
        spread(m, 1)
    vec_step(3)
    for m in late:
        spread(m, 2)

    for q in halo_back:
        q.wait()
    grad_sent = r.gext[RIM : RIM + ROWS] + r.rims[2:4].reshape(ROWS, D).astype(F32)
    rcopy(r.pk2.at[pl.ds(0, DEVICES - 1)], r.arr2.at[pl.ds(0, DEVICES - 1)], r.as2, r.ar2, west).wait()

    @pl.loop(0, 8)
    def _(j):
        r.arr_n[pl.ds(pl.multiple_of(j * 128, 128), 128)] = from_pairs(r.arr2[pl.ds(j * 16, 16)])

    grad_sent += mm(sub_hot(r.csend[...], ROWS), r.arr_n[...])
    up = (r.gnb[...] + mm_bt(grad_sent.astype(BF16), r.sw[...])) * r.ngain[...]
    h = r.lhat[...]
    back = r.linv[...] * (up - mean_row(up) - h * mean_row(up * h))
    r.glat[...] = (r.cot[...].astype(F32) + back).astype(BF16)

    for m in late:
        spread(m, 1)
    for m in range(6):
        ag_core(m).wait()


def widen(sums, *outs):
    for out, m in zip(outs, (SEND, RECEIVE, EDGE, NODE_SELF, NODE_OUT)):
        if m == NODE_SELF:
            out[...] = sums[m : m + 2].astype(F32)
        else:
            out[...] = sums[m].astype(F32)


def per_device(
    latents, near_index, coarse_slot, coarse_send, norm_gain, send_weight, receive_weight, edge_bias,
    edge_weight, edge_gain, node_input, node_bias, node_output, cotangent,
):
    whole = pl.BlockSpec(memory_space=pltpu.VMEM)
    new_latents, grad_latents, sums, vectors = pl.pallas_call(
        body,
        out_shape=(
            jax.ShapeDtypeStruct((ROWS, D), BF16),
            jax.ShapeDtypeStruct((ROWS, D), BF16),
            jax.ShapeDtypeStruct((6, D, D), BF16),
            jax.ShapeDtypeStruct((4, D), F32),
        ),
        in_specs=[whole] * 14,
        out_specs=(whole,) * 4,
        scratch_shapes=list(scratch().values()),
        compiler_params=pltpu.CompilerParams(
            collective_id=0, has_side_effects=True, vmem_limit_bytes=58 * 2**20
        ),
    )(
        latents, near_index, coarse_slot, coarse_send, norm_gain.reshape(1, D), send_weight, receive_weight,
        edge_bias.reshape(1, D), edge_weight, edge_gain.reshape(1, D), node_input, node_bias.reshape(1, D),
        node_output, cotangent,
    )
    rows = 128
    square = pl.BlockSpec((rows, D), lambda i: (i, 0))
    twice = pl.BlockSpec((2, rows, D), lambda i: (0, i, 0))
    one = jax.ShapeDtypeStruct((D, D), F32)
    send, receive, edge, node_in, node_out = pl.pallas_call(
        widen,
        grid=(D // rows,),
        out_shape=(one, one, one, jax.ShapeDtypeStruct((2, D, D), F32), one),
        in_specs=[pl.BlockSpec((6, rows, D), lambda i: (0, i, 0))],
        out_specs=(square, square, square, twice, square),
    )(sums)
    return new_latents, grad_latents, send, receive, edge, node_in.reshape(2 * D, D), node_out, vectors


def solution(mesh):
    rows, whole = P(("lat", "lon"), None), P()
    split = P(None, ("lat", "lon"))
    return jax.shard_map(
        per_device,
        mesh=mesh,
        in_specs=(rows, split, split, rows) + (whole,) * 9 + (rows,),
        out_specs=(rows, rows) + (whole,) * 6,
        check_vma=False,
    )
```

```python
import types

import jax
import jax.numpy as jnp
from jax import lax
from jax.experimental import pallas as pl
from jax.experimental.pallas import tpu as pltpu
from jax.sharding import PartitionSpec as P

MESH = pl.DeviceIdType.MESH
EPS = 1e-05
D = 512
ROWS = 256
RIM = 128
DEG = 4
CDEG = 2
EDGES = DEG + CDEG
DEVICES = 128
CAP = 8
SLOTS = DEVICES * CAP
F32 = jnp.float32
BF16 = jnp.bfloat16

NODE_OUT, NODE_SELF, NODE_AGG, RECEIVE, EDGE, SEND = range(6)


def exchange_order():
    cube = [(i, j, k) for i in range(4) for j in range(4) for k in range(4)]
    cube.sort(key=lambda d: (-sum(min(v, 4 - v) for v in d), [-v for v in d]))
    order = []
    for d in cube:
        for sign in (1, -1):
            for turn in range(3):
                e = tuple((sign * v) % 4 for v in d[turn:] + d[:turn])
                if e not in order:
                    order.append(e)
    return [e + (core,) for e in order for core in (0, 1) if any(e) or core]


ORDER = exchange_order()
FIRST, SECOND, THIRD = 32, 64, 96


def mm(a, b):
    return jnp.dot(a, b, preferred_element_type=F32)


def mm_bt(a, b):
    return lax.dot_general(a, b, (((1,), (1,)), ((), ())), preferred_element_type=F32)


def mm_at(a, b):
    return lax.dot_general(a, b, (((0,), (0,)), ((), ())), preferred_element_type=F32)


def mean_row(v):
    return jnp.mean(v, axis=-1, keepdims=True)


def silu_parts(v):
    gate = 0.5 * jnp.tanh(0.5 * v) + 0.5
    out = v * gate
    return out, gate + out * (1.0 - gate)


def norm_rows(v):
    centred = v - mean_row(v)
    inverse = lax.rsqrt(mean_row(centred * centred) + EPS)
    return centred * inverse, inverse


def col_sum(v):
    return jnp.sum(v, axis=0, keepdims=True)


def lane_hot(column, width):
    lanes = lax.broadcasted_iota(jnp.int32, (column.shape[0], width), 1)
    return jnp.where(lanes == column, 1.0, 0.0).astype(BF16)


def sub_hot(row, height):
    subs = lax.broadcasted_iota(jnp.int32, (height, row.shape[1]), 0)
    return jnp.where(subs == row, 1.0, 0.0).astype(BF16)


def to_pairs(rows):
    k = rows.shape[0] // CAP
    left = rows[:, : D // 2].reshape(k, CAP, D // 2)
    right = rows[:, D // 2 :].reshape(k, CAP, D // 2)
    return jnp.concatenate([left, right], axis=1).astype(BF16)


def from_pairs(pairs):
    k = pairs.shape[0]
    wide = pairs.astype(F32)
    left = wide[:, :CAP].reshape(k * CAP, D // 2)
    right = wide[:, CAP:].reshape(k * CAP, D // 2)
    return jnp.concatenate([left, right], axis=1).astype(BF16)


INPUTS = ["lat", "near", "slot", "csend", "ngain", "sw", "rw", "ebias", "ew", "egain", "ni", "nbias", "no", "cot"]
OUTPUTS = ["newlat", "glat", "res", "vout"]


def scratch():
    dma = pltpu.SemaphoreType.DMA
    half = (DEVICES, 2 * CAP, D // 2)
    square = pltpu.VMEM((D, D), BF16)
    row = pltpu.VMEM((1, D), F32)
    return {
        "lat": pltpu.VMEM((ROWS, D), BF16),
        "near": pltpu.VMEM((DEG, ROWS), jnp.int32),
        "slot": pltpu.VMEM((CDEG, ROWS), jnp.int32),
        "csend": pltpu.VMEM((1, SLOTS), jnp.int32),
        "ngain": row, "sw": square, "rw": square, "ebias": row, "ew": square, "egain": row,
        "ni": pltpu.VMEM((2 * D, D), BF16),
        "nbias": row, "no": square,
        "cot": pltpu.VMEM((ROWS, D), BF16),
        "loads": dma((14,)),
        "newlat": pltpu.VMEM((ROWS, D), BF16),
        "glat": pltpu.VMEM((ROWS, D), BF16),
        "res": pltpu.VMEM((6, D, D), BF16),
        "vout": pltpu.VMEM((4, D), F32),
        "stores": dma((15,)),
        "ext_n": pltpu.VMEM((ROWS + 2 * RIM, D), BF16),
        "lhat": pltpu.VMEM((ROWS, D), F32),
        "linv": pltpu.VMEM((ROWS, 1), F32),
        "pk": pltpu.VMEM(half, BF16),
        "arr": pltpu.VMEM(half, BF16),
        "pk2": pltpu.VMEM(half, BF16),
        "arr2": pltpu.VMEM(half, BF16),
        "arr_n": pltpu.VMEM((SLOTS, D), BF16),
        "cols": pltpu.VMEM((EDGES, ROWS, 1), jnp.int32),
        "recv": pltpu.VMEM((ROWS, D), F32),
        "gh": pltpu.VMEM((ROWS, D), F32),
        "npre": pltpu.VMEM((ROWS, D), F32),
        "sent_ext": pltpu.VMEM((ROWS + 2 * RIM, D), BF16),
        "act": pltpu.VMEM((EDGES, ROWS, D), BF16),
        "slope": pltpu.VMEM((EDGES, ROWS, D), F32),
        "hat": pltpu.VMEM((EDGES, ROWS, D), F32),
        "einv": pltpu.VMEM((EDGES, ROWS, 1), F32),
        "hsum": pltpu.VMEM((ROWS, D), F32),
        "cn": pltpu.VMEM((CDEG, ROWS, D), BF16),
        "geb": pltpu.VMEM((EDGES, ROWS, D), BF16),
        "gext": pltpu.VMEM((ROWS + 2 * RIM, D), F32),
        "rims": pltpu.VMEM((4, RIM, D), BF16),
        "gnp": pltpu.VMEM((ROWS, D), BF16),
        "aggr": pltpu.VMEM((ROWS, D), BF16),
        "grecv": pltpu.VMEM((ROWS, D), BF16),
        "gnb": pltpu.VMEM((ROWS, D), F32),
        "acc": pltpu.VMEM((D, D), F32),
        "part": pltpu.VMEM((6, D, D), BF16),
        "crecv": pltpu.VMEM((6, D // 2, D), BF16),
        "s1": pltpu.VMEM((6, D // 2, D), BF16),
        "r1": pltpu.VMEM((6, 3, D // 8, D), BF16),
        "s2": pltpu.VMEM((6, D // 8, D), BF16),
        "r2": pltpu.VMEM((6, 3, D // 32, D), BF16),
        "r3": pltpu.VMEM((6, 4, D // 32, D), BF16),
        "vec": pltpu.VMEM((4, 8, D), F32),
        "vrecv": pltpu.VMEM((4, 4, 8, D), F32),
        "hs": dma((2,)), "hr": dma((2,)), "hs2": dma((2,)), "hr2": dma((2,)),
        "as_": dma, "ar": dma, "as2": dma, "ar2": dma,
        "cs": dma((6,)), "cr": dma((6,)), "gcs": dma((6,)), "gcr": dma((6,)),
        "s1s": dma((6, 3)), "s1r": dma((6, 3)), "s2s": dma((6, 3)), "s2r": dma((6, 3)),
        "s3s": dma((6, 3)), "s3r": dma((6, 3)), "g1s": dma((6, 3)), "g1r": dma((6, 3)),
        "g2s": dma((6, 3)), "g2r": dma((6, 3)),
        "vs": dma((4, 3)), "vr": dma((4, 3)),
    }


def body(*refs):
    names = ["in_" + n for n in INPUTS] + ["out_" + n for n in OUTPUTS] + list(scratch())
    r = types.SimpleNamespace(**dict(zip(names, refs)))
    la = lax.axis_index("lat")
    lo = lax.axis_index("lon")
    me = la * 32 + lo
    z, y, x, c = la, lo // 8, lax.rem(lo // 2, 4), lax.rem(lo, 2)

    def at(z, y, x, c):
        return (z, y * 8 + x * 2 + c)

    coord = {"x": x, "y": y, "z": z}

    def peer(axis, d):
        p = dict(coord)
        p[axis] = lax.rem(coord[axis] + d, 4)
        return at(p["z"], p["y"], p["x"], c), p[axis]

    def rcopy(src, dst, ssem, rsem, device):
        return pltpu.make_async_remote_copy(src, dst, ssem, rsem, device_id=device, device_id_type=MESH)

    orders = {m: ("xyz", "yzx", "zxy")[m % 3] for m in range(6)}
    scale = float(ROWS * DEVICES) ** -0.5
    other = at(z, y, x, 1 - c)

    def half(core):
        return pl.ds(pl.multiple_of(core * 256, 256), 256)

    def core_copy(m):
        return rcopy(r.part.at[m, half(1 - c)], r.crecv.at[m], r.cs.at[m], r.cr.at[m], other)

    def rs1(m, d):
        device, pos = peer(orders[m][0], d)
        rows = pl.ds(pl.multiple_of(pos * 64, 64), 64)
        return rcopy(r.s1.at[m, rows], r.r1.at[m, d - 1], r.s1s.at[m, d - 1], r.s1r.at[m, d - 1], device)

    def rs2(m, d):
        device, pos = peer(orders[m][1], d)
        rows = pl.ds(pl.multiple_of(pos * 16, 16), 16)
        return rcopy(r.s2.at[m, rows], r.r2.at[m, d - 1], r.s2s.at[m, d - 1], r.s2r.at[m, d - 1], device)

    def swap3(m, d):
        device, _ = peer(orders[m][2], d)
        return rcopy(r.r3.at[m, 0], r.r3.at[m, d], r.s3s.at[m, d - 1], r.s3r.at[m, d - 1], device)

    def spot(m, level):
        a, b = coord[orders[m][0]] * 64, coord[orders[m][1]] * 16
        if level == 2:
            return r.res.at[m, pl.ds(pl.multiple_of(c * 256 + a + b, 16), 16)]
        if level == 1:
            return r.res.at[m, pl.ds(pl.multiple_of(c * 256 + a, 64), 64)]
        return r.res.at[m, half(c)]

    def ag(m, level, d):
        ssem, rsem = {2: (r.g2s, r.g2r), 1: (r.g1s, r.g1r)}[level]
        device, _ = peer(orders[m][level - 1], d)
        return rcopy(spot(m, level), spot(m, level), ssem.at[m, d - 1], rsem.at[m, d - 1], device)

    def ag_core(m):
        return rcopy(spot(m, 0), spot(m, 0), r.gcs.at[m], r.gcr.at[m], other)

    def fold_core(m):
        core_copy(m).wait()
        r.s1[m] = (r.part[m, half(c)].astype(F32) + r.crecv[m].astype(F32)).astype(BF16)
        for d in (2, 1, 3):
            rs1(m, d).start()

    def fold1(m):
        total = r.s1[m, pl.ds(pl.multiple_of(coord[orders[m][0]] * 64, 64), 64)].astype(F32)
        for d in (1, 3, 2):
            rs1(m, d).wait()
            total += r.r1[m, d - 1].astype(F32)
        r.s2[m] = total.astype(BF16)
        for d in (2, 1, 3):
            rs2(m, d).start()

    def fold2(m):
        total = r.s2[m, pl.ds(pl.multiple_of(coord[orders[m][1]] * 16, 16), 16)].astype(F32)
        for d in (1, 3, 2):
            rs2(m, d).wait()
            total += r.r2[m, d - 1].astype(F32)
        r.r3[m, 0] = total.astype(BF16)
        for d in (2, 1, 3):
            swap3(m, d).start()

    def fold3(m):
        for d in (1, 3, 2):
            swap3(m, d).wait()
        total = jnp.zeros((16, D), F32)
        for i in range(4):
            total += r.r3[m, lax.rem(coord[orders[m][2]] - i + 4, 4)].astype(F32)
        spot(m, 2)[...] = (total * scale).astype(BF16)
        for d in (2, 1, 3):
            ag(m, 2, d).start()

    def spread(m, level):
        for d in (1, 3, 2):
            ag(m, level, d).wait()
        if level == 2:
            for d in (2, 1, 3):
                ag(m, 1, d).start()
        else:
            ag_core(m).start()
            store(r.res.at[m, half(c)], r.out_res.at[m, half(c)])

    def vec_copies(level):
        if level == 0:
            return [rcopy(r.vec.at[0], r.vrecv.at[0, 1], r.vs.at[0, 0], r.vr.at[0, 0], other)]
        return [
            rcopy(r.vec.at[level], r.vrecv.at[level, d], r.vs.at[level, d - 1], r.vr.at[level, d - 1], peer("xyz"[level - 1], d)[0])
            for d in (1, 2, 3)
        ]

    def vec_step(level):
        for q in vec_copies(level):
            q.wait()
        if level == 0:
            total = r.vec[0] + r.vrecv[0, 1]
        else:
            r.vrecv[level, 0] = r.vec[level]
            total = jnp.zeros((8, D), F32)
            for i in range(4):
                total += r.vrecv[level, lax.rem(coord["xyz"[level - 1]] - i + 4, 4)]
        if level < 3:
            r.vec[level + 1] = total
            for q in vec_copies(level + 1):
                q.start()
        else:
            r.vout[...] = total[0:4] * scale
            store(r.vout, r.out_vout)

    bar = pltpu.get_barrier_semaphore()

    zs = [lax.rem(z + i, 4) for i in range(4)]
    ys = [lax.rem(y + i, 4) * 8 for i in range(4)]
    xs = [lax.rem(x + i, 4) * 2 for i in range(4)]
    cores = [c, 1 - c]

    def away(d):
        return (zs[d[0]], ys[d[1]] + xs[d[2]] + cores[d[3]])

    for d in ORDER:
        pl.semaphore_signal(bar, inc=1, device_id=away(d), device_id_type=MESH)

    def load(name):
        return pltpu.make_async_copy(getattr(r, "in_" + name), getattr(r, name), r.loads.at[INPUTS.index(name)])

    def need(*wanted):
        for name in wanted:
            load(name).wait()

    stores = []

    def store(source, target):
        copy = pltpu.make_async_copy(source, target, r.stores.at[len(stores)])
        copy.start()
        stores.append(copy)

    for name in ("lat", "ngain", "csend", "near", "slot", "rw", "ebias", "sw", "cot", "no", "ni", "nbias", "ew", "egain"):
        load(name).start()
    need("lat", "ngain", "csend", "near", "slot")

    h, inv = norm_rows(r.lat[...].astype(F32))
    r.lhat[...] = h
    r.linv[...] = inv
    r.ext_n[RIM : RIM + ROWS] = (h * r.ngain[...]).astype(BF16)

    idx = jnp.concatenate([r.near[...], r.slot[...], jnp.zeros((2, ROWS), jnp.int32)], axis=0)
    idx_t = jnp.transpose(idx)
    for k in range(EDGES):
        r.cols[k] = idx_t[:, k : k + 1]
    send_t = jnp.transpose(r.csend[...].reshape(8, 128))
    for j in range(8):
        rows = mm(lane_hot(send_t[:, j : j + 1], ROWS), r.ext_n[RIM : RIM + ROWS])
        r.pk[16 * j : 16 * j + 16] = to_pairs(rows)

    pl.semaphore_wait(bar, DEVICES - 1)

    west = (la, lax.rem(lo + 31, 32))
    east = (la, lax.rem(lo + 1, 32))
    halo = [
        rcopy(r.ext_n.at[pl.ds(2 * RIM, RIM)], r.ext_n.at[pl.ds(0, RIM)], r.hs.at[0], r.hr.at[0], east),
        rcopy(r.ext_n.at[pl.ds(RIM, RIM)], r.ext_n.at[pl.ds(3 * RIM, RIM)], r.hs.at[1], r.hr.at[1], west),
    ]
    for q in halo:
        q.start()

    for d in ORDER:
        t = away(d)
        rcopy(r.pk.at[t[0] * 32 + t[1]], r.arr.at[me], r.as_, r.ar, t).start()

    r.arr[me] = r.pk[me]

    need("rw", "ebias", "sw", "cot", "no", "ni", "nbias", "ew", "egain")

    def own():
        return r.ext_n[RIM : RIM + ROWS]

    r.recv[...] = mm(own(), r.rw[...]) + r.ebias[...]
    r.sent_ext[RIM : RIM + ROWS] = mm(own(), r.sw[...]).astype(BF16)
    r.gh[...] = mm_bt(r.cot[...], r.no[...])
    r.npre[...] = mm(own(), r.ni[0:D]) + r.nbias[...]
    r.hsum[...] = jnp.zeros((ROWS, D), F32)
    for q in halo:
        q.wait()
    r.sent_ext[0:RIM] = mm(r.ext_n[0:RIM], r.sw[...]).astype(BF16)
    r.sent_ext[3 * RIM : 4 * RIM] = mm(r.ext_n[3 * RIM : 4 * RIM], r.sw[...]).astype(BF16)

    def edge_forward(k, senders):
        a, s = silu_parts(senders + r.recv[...])
        a = a.astype(BF16)
        r.act[k] = a
        r.slope[k] = s
        h, inv = norm_rows(mm(a, r.ew[...]))
        r.hat[k] = h
        r.einv[k] = inv
        r.hsum[...] += h

    @pl.loop(0, DEG)
    def _(k):
        edge_forward(k, mm(lane_hot(r.cols[k], ROWS + 2 * RIM), r.sent_ext[...]))

    everything = rcopy(r.pk.at[pl.ds(0, DEVICES - 1)], r.arr.at[pl.ds(0, DEVICES - 1)], r.as_, r.ar, west)
    everything.wait()

    @pl.loop(0, 8)
    def _(j):
        r.arr_n[pl.ds(pl.multiple_of(j * 128, 128), 128)] = from_pairs(r.arr[pl.ds(j * 16, 16)])

    @pl.loop(0, CDEG)
    def _(k):
        rows = mm(lane_hot(r.cols[DEG + k], SLOTS), r.arr_n[...]).astype(BF16)
        r.cn[k] = rows
        edge_forward(DEG + k, mm(rows, r.sw[...]).astype(BF16).astype(F32))

    aggregate = (r.hsum[...] * r.egain[...]).astype(BF16)
    hidden, node_slope = silu_parts(r.npre[...] + mm(aggregate, r.ni[D : 2 * D]))
    hidden = hidden.astype(BF16)
    r.newlat[...] = (r.lat[...].astype(F32) + mm(hidden, r.no[...])).astype(BF16)
    store(r.newlat, r.out_newlat)
    gnp = (r.gh[...] * node_slope).astype(BF16)
    r.gnp[...] = gnp
    r.aggr[...] = aggregate
    gagg = mm_bt(gnp, r.ni[D : 2 * D])
    r.vec[0] = jnp.zeros((8, D), F32)
    r.vec[0, 2:3] = col_sum(gagg * r.hsum[...])
    r.vec[0, 3:4] = col_sum(gnp.astype(F32))
    r.part[NODE_OUT] = mm_at(hidden, r.cot[...]).astype(BF16)
    r.part[NODE_SELF] = mm_at(own(), r.gnp[...]).astype(BF16)

    r.part[NODE_AGG] = mm_at(r.aggr[...], r.gnp[...]).astype(BF16)
    early, late = (NODE_OUT, NODE_SELF, NODE_AGG), (RECEIVE, EDGE, SEND)
    for m in early:
        core_copy(m).start()

    up = gagg * r.egain[...]
    r.npre[...] = up - mean_row(up)
    r.gh[...] = up
    r.recv[...] = jnp.zeros((ROWS, D), F32)
    r.acc[...] = jnp.zeros((D, D), F32)

    def edge_backward(k):
        h = r.hat[k]
        g = (r.einv[k] * (r.npre[...] - h * mean_row(r.gh[...] * h))).astype(BF16)
        ge = mm_bt(g, r.ew[...]) * r.slope[k]
        r.recv[...] += ge
        r.geb[k] = ge.astype(BF16)
        r.acc[...] += mm_at(r.act[k], g)

    pl.loop(DEG, EDGES)(edge_backward)
    for j in range(4):
        block = jnp.zeros((256, D), F32)
        for k in range(CDEG):
            block += mm(sub_hot(r.slot[k : k + 1, :] - 256 * j, 256), r.geb[DEG + k])
        r.pk2[32 * j : 32 * j + 32] = to_pairs(block)
    r.arr2[me] = r.pk2[me]

    def send_back(first, last):
        for d in ORDER[first:last]:
            t = away(d)
            rcopy(r.pk2.at[t[0] * 32 + t[1]], r.arr2.at[me], r.as2, r.ar2, t).start()

    send_back(0, FIRST)
    for m in early:
        fold_core(m)
    pl.loop(0, DEG)(edge_backward)

    r.part[EDGE] = r.acc[...].astype(BF16)
    core_copy(EDGE).start()
    r.grecv[...] = r.recv[...].astype(BF16)
    r.part[RECEIVE] = mm_at(own(), r.grecv[...]).astype(BF16)
    core_copy(RECEIVE).start()
    for j in range(4):
        block = jnp.zeros((RIM, D), F32)
        for k in range(DEG):
            block += mm(sub_hot(r.near[k : k + 1, :] - RIM * j, RIM), r.geb[k])
        r.gext[RIM * j : RIM * j + RIM] = block
    r.acc[...] = mm_at(r.ext_n[...], r.gext[...].astype(BF16))
    for k in range(CDEG):
        r.acc[...] += mm_at(r.cn[k], r.geb[DEG + k])
    r.part[SEND] = r.acc[...].astype(BF16)
    core_copy(SEND).start()
    for m in early:
        fold1(m)
    for m in (EDGE, RECEIVE, SEND):
        fold_core(m)

    r.rims[0] = r.gext[0:RIM].astype(BF16)
    r.rims[1] = r.gext[3 * RIM : 4 * RIM].astype(BF16)
    halo_back = [
        rcopy(r.rims.at[1], r.rims.at[2], r.hs2.at[0], r.hr2.at[0], east),
        rcopy(r.rims.at[0], r.rims.at[3], r.hs2.at[1], r.hr2.at[1], west),
    ]
    for q in halo_back:
        q.start()
    local_back = mm_bt(r.gnp[...], r.ni[0:D]) + mm_bt(r.grecv[...], r.rw[...])
    r.gnb[...] = local_back
    through_sent = jnp.sum(r.sw[...].astype(F32) * r.acc[...], axis=1, keepdims=True)
    through_sent = jnp.transpose(jnp.broadcast_to(through_sent, (D, 128)))[0:1]
    r.vec[0, 0:1] = col_sum(r.lhat[...] * local_back) + through_sent / r.ngain[...]
    r.vec[0, 1:2] = col_sum(r.recv[...])
    for q in vec_copies(0):
        q.start()

    for m in early:
        fold2(m)
    vec_step(0)
    send_back(FIRST, SECOND)
    for m in late:
        fold1(m)
    for m in early:
        fold3(m)
    send_back(SECOND, THIRD)
    vec_step(1)
    for m in late:
        fold2(m)
    for m in early:
        spread(m, 2)
    send_back(THIRD, DEVICES - 1)
    vec_step(2)
    for m in late:
        fold3(m)
    for m in early:
        spread(m, 1)
    vec_step(3)
    for m in late:
        spread(m, 2)

    for q in halo_back:
        q.wait()
    grad_sent = r.gext[RIM : RIM + ROWS] + r.rims[2:4].reshape(ROWS, D).astype(F32)
    rcopy(r.pk2.at[pl.ds(0, DEVICES - 1)], r.arr2.at[pl.ds(0, DEVICES - 1)], r.as2, r.ar2, west).wait()

    @pl.loop(0, 8)
    def _(j):
        r.arr_n[pl.ds(pl.multiple_of(j * 128, 128), 128)] = from_pairs(r.arr2[pl.ds(j * 16, 16)])

    grad_sent += mm(sub_hot(r.csend[...], ROWS), r.arr_n[...])
    up = (r.gnb[...] + mm_bt(grad_sent.astype(BF16), r.sw[...])) * r.ngain[...]
    h = r.lhat[...]
    back = r.linv[...] * (up - mean_row(up) - h * mean_row(up * h))
    r.glat[...] = (r.cot[...].astype(F32) + back).astype(BF16)
    store(r.glat, r.out_glat)

    for m in late:
        spread(m, 1)
    for m in range(6):
        ag_core(m).wait()
        store(r.res.at[m, half(1 - c)], r.out_res.at[m, half(1 - c)])
    for copy in stores:
        copy.wait()


def widen(sums, newlat, glat, vectors, *refs):
    outs, narrow, wide, rows, vec, in_sems, out_sems = refs[:8], *refs[8:]
    loads = [pltpu.make_async_copy(sums.at[m], narrow.at[m], in_sems.at[m]) for m in range(6)]
    through = ((newlat, rows.at[0], outs[0]), (glat, rows.at[1], outs[1]), (vectors, vec, outs[7]))
    for i, (source, held, _) in enumerate(through):
        loads.append(pltpu.make_async_copy(source, held, in_sems.at[6 + i]))
    for copy in loads:
        copy.start()
    stores = []

    def store(source, target):
        copy = pltpu.make_async_copy(source, target, out_sems.at[len(stores)])
        copy.start()
        stores.append(copy)

    targets = {
        SEND: outs[2], RECEIVE: outs[3], EDGE: outs[4], NODE_OUT: outs[6],
        NODE_SELF: outs[5].at[pl.ds(0, D)], NODE_AGG: outs[5].at[pl.ds(D, D)],
    }
    for m in range(6):
        loads[m].wait()
        wide[m] = narrow[m].astype(F32)
        store(wide.at[m], targets[m])
    for i, (_, held, target) in enumerate(through):
        loads[6 + i].wait()
        store(held, target)
    for copy in stores:
        copy.wait()


def per_device(
    latents, near_index, coarse_slot, coarse_send, norm_gain, send_weight, receive_weight, edge_bias,
    edge_weight, edge_gain, node_input, node_bias, node_output, cotangent,
):
    whole = pl.BlockSpec(memory_space=pltpu.HBM)
    new_latents, grad_latents, sums, vectors = pl.pallas_call(
        body,
        out_shape=(
            jax.ShapeDtypeStruct((ROWS, D), BF16),
            jax.ShapeDtypeStruct((ROWS, D), BF16),
            jax.ShapeDtypeStruct((6, D, D), BF16),
            jax.ShapeDtypeStruct((4, D), F32),
        ),
        in_specs=[whole] * 14,
        out_specs=(whole,) * 4,
        scratch_shapes=list(scratch().values()),
        compiler_params=pltpu.CompilerParams(
            collective_id=0, has_side_effects=True, vmem_limit_bytes=58 * 2**20
        ),
    )(
        latents, near_index, coarse_slot, coarse_send, norm_gain.reshape(1, D), send_weight, receive_weight,
        edge_bias.reshape(1, D), edge_weight, edge_gain.reshape(1, D), node_input, node_bias.reshape(1, D),
        node_output, cotangent,
    )
    shard, one = jax.ShapeDtypeStruct((ROWS, D), BF16), jax.ShapeDtypeStruct((D, D), F32)
    return pl.pallas_call(
        widen,
        out_shape=(
            shard, shard, one, one, one, jax.ShapeDtypeStruct((2 * D, D), F32), one,
            jax.ShapeDtypeStruct((4, D), F32),
        ),
        in_specs=[whole] * 4,
        out_specs=(whole,) * 8,
        scratch_shapes=[
            pltpu.VMEM((6, D, D), BF16), pltpu.VMEM((6, D, D), F32),
            pltpu.VMEM((2, ROWS, D), BF16), pltpu.VMEM((4, D), F32),
            pltpu.SemaphoreType.DMA((9,)), pltpu.SemaphoreType.DMA((9,)),
        ],
        compiler_params=pltpu.CompilerParams(vmem_limit_bytes=58 * 2**20),
    )(sums, new_latents, grad_latents, vectors)


def solution(mesh):
    rows, whole = P(("lat", "lon"), None), P()
    split = P(None, ("lat", "lon"))
    return jax.shard_map(
        per_device,
        mesh=mesh,
        in_specs=(rows, split, split, rows) + (whole,) * 9 + (rows,),
        out_specs=(rows, rows) + (whole,) * 6,
        check_vma=False,
    )
```

```python
import types

import jax
import jax.numpy as jnp
from jax import lax
from jax.experimental import pallas as pl
from jax.experimental.pallas import tpu as pltpu
from jax.sharding import PartitionSpec as P

MESH = pl.DeviceIdType.MESH
EPS = 1e-05
D = 512
ROWS = 256
RIM = 128
DEG = 4
CDEG = 2
EDGES = DEG + CDEG
DEVICES = 128
CAP = 8
SLOTS = DEVICES * CAP
EXT = ROWS + 2 * RIM
F32 = jnp.float32
BF16 = jnp.bfloat16

NODE_OUT, NODE_SELF, NODE_AGG, RECEIVE, EDGE, SEND = range(6)


def exchange_order():
    cube = [(i, j, k) for i in range(4) for j in range(4) for k in range(4)]
    cube.sort(key=lambda d: (-sum(min(v, 4 - v) for v in d), [-v for v in d]))
    order = []
    for d in cube:
        for sign in (1, -1):
            for turn in range(3):
                e = tuple((sign * v) % 4 for v in d[turn:] + d[:turn])
                if e not in order:
                    order.append(e)
    return [e + (core,) for e in order for core in (0, 1) if any(e) or core]


ORDER = exchange_order()
FIRST, SECOND, THIRD = 64, 85, 106


def mm(a, b):
    return jnp.dot(a, b, preferred_element_type=F32)


def mm_bt(a, b):
    return lax.dot_general(a, b, (((1,), (1,)), ((), ())), preferred_element_type=F32)


def mm_at(a, b):
    return lax.dot_general(a, b, (((0,), (0,)), ((), ())), preferred_element_type=F32)


def mean_row(v):
    return jnp.mean(v, axis=-1, keepdims=True)


def silu_parts(v):
    gate = 0.5 * jnp.tanh(0.5 * v) + 0.5
    out = v * gate
    return out, gate + out * (1.0 - gate)


def norm_rows(v):
    centred = v - mean_row(v)
    inverse = lax.rsqrt(mean_row(centred * centred) + EPS)
    return centred * inverse, inverse


def col_sum(v):
    return jnp.sum(v, axis=0, keepdims=True)


def lane_hot(column, width):
    lanes = lax.broadcasted_iota(jnp.int32, (column.shape[0], width), 1)
    return jnp.where(lanes == column, 1.0, 0.0).astype(BF16)


def sub_hot(row, height):
    subs = lax.broadcasted_iota(jnp.int32, (height, row.shape[1]), 0)
    return jnp.where(subs == row, 1.0, 0.0).astype(BF16)


def to_pairs(rows):
    k = rows.shape[0] // CAP
    left = rows[:, : D // 2].reshape(k, CAP, D // 2)
    right = rows[:, D // 2 :].reshape(k, CAP, D // 2)
    return jnp.concatenate([left, right], axis=1).astype(BF16)


def from_pairs(pairs):
    k = pairs.shape[0]
    wide = pairs.astype(F32)
    left = wide[:, :CAP].reshape(k * CAP, D // 2)
    right = wide[:, CAP:].reshape(k * CAP, D // 2)
    return jnp.concatenate([left, right], axis=1).astype(BF16)


INPUTS = ["lat", "near", "slot", "csend", "ngain", "sw", "rw", "ebias", "ew", "egain", "ni", "nbias", "no", "cot"]
OUTPUTS = ["newlat", "glat", "res", "vout"]


def scratch():
    dma = pltpu.SemaphoreType.DMA
    half = (DEVICES, 2 * CAP, D // 2)
    square = pltpu.VMEM((D, D), BF16)
    row = pltpu.VMEM((1, D), F32)
    return {
        "lat": pltpu.VMEM((ROWS, D), BF16),
        "near": pltpu.VMEM((DEG, ROWS), jnp.int32),
        "slot": pltpu.VMEM((CDEG, ROWS), jnp.int32),
        "csend": pltpu.VMEM((1, SLOTS), jnp.int32),
        "ngain": row, "sw": square, "rw": square, "ebias": row, "ew": square, "egain": row,
        "ni": pltpu.VMEM((2 * D, D), BF16),
        "nbias": row, "no": square,
        "cot": pltpu.VMEM((ROWS, D), BF16),
        "loads": dma((14,)),
        "newlat": pltpu.VMEM((ROWS, D), BF16),
        "glat": pltpu.VMEM((ROWS, D), BF16),
        "res": pltpu.VMEM((6, D, D), BF16),
        "vout": pltpu.VMEM((4, D), F32),
        "stores": dma((15,)),
        "ext_n": pltpu.VMEM((EXT + CDEG * ROWS, D), BF16),
        "lhat": pltpu.VMEM((ROWS, D), F32),
        "linv": pltpu.VMEM((ROWS, 1), F32),
        "pk": pltpu.VMEM(half, BF16),
        "arr": pltpu.VMEM(half, BF16),
        "pk2": pltpu.VMEM(half, BF16),
        "arr2": pltpu.VMEM(half, BF16),
        "arr_n": pltpu.VMEM((SLOTS, D), BF16),
        "cols": pltpu.VMEM((EDGES, ROWS, 1), jnp.int32),
        "recv": pltpu.VMEM((ROWS, D), F32),
        "gh": pltpu.VMEM((ROWS, D), F32),
        "npre": pltpu.VMEM((ROWS, D), F32),
        "sent_ext": pltpu.VMEM((ROWS + 2 * RIM, D), BF16),
        "act": pltpu.VMEM((EDGES, ROWS, D), BF16),
        "slope": pltpu.VMEM((EDGES, ROWS, D), F32),
        "hat": pltpu.VMEM((EDGES, ROWS, D), F32),
        "einv": pltpu.VMEM((EDGES, ROWS, 1), F32),
        "hsum": pltpu.VMEM((ROWS, D), F32),
        "gsend": pltpu.VMEM((EXT + CDEG * ROWS, D), BF16),
        "gpre": pltpu.VMEM((EDGES, ROWS, D), BF16),
        "geb": pltpu.VMEM((DEG, ROWS, D), BF16),
        "gext": pltpu.VMEM((ROWS + 2 * RIM, D), F32),
        "rims": pltpu.VMEM((2, RIM, D), BF16),
        "gnp": pltpu.VMEM((ROWS, D), BF16),
        "hidden": pltpu.VMEM((ROWS, D), BF16),
        "aggr": pltpu.VMEM((ROWS, D), BF16),
        "grecv": pltpu.VMEM((ROWS, D), BF16),
        "gnb": pltpu.VMEM((ROWS, D), F32),
        "acc": pltpu.VMEM((D, D), F32),
        "part": pltpu.VMEM((6, D, D), BF16),
        "crecv": pltpu.VMEM((6, D // 2, D), BF16),
        "s1": pltpu.VMEM((6, D // 2, D), BF16),
        "r1": pltpu.VMEM((6, 3, D // 8, D), BF16),
        "s2": pltpu.VMEM((6, D // 8, D), BF16),
        "r2": pltpu.VMEM((6, 3, D // 32, D), BF16),
        "r3": pltpu.VMEM((6, 4, D // 32, D), BF16),
        "vec": pltpu.VMEM((4, 8, D), F32),
        "vrecv": pltpu.VMEM((4, 4, 8, D), F32),
        "hs": dma((2,)), "hr": dma((2,)), "hs2": dma((2,)), "hr2": dma((2,)),
        "as_": dma, "ar": dma, "as2": dma, "ar2": dma,
        "cs": dma((6,)), "cr": dma((6,)), "gcs": dma((6,)), "gcr": dma((6,)),
        "s1s": dma((6, 3)), "s1r": dma((6, 3)), "s2s": dma((6, 3)), "s2r": dma((6, 3)),
        "s3s": dma((6, 3)), "s3r": dma((6, 3)), "g1s": dma((6, 3)), "g1r": dma((6, 3)),
        "g2s": dma((6, 3)), "g2r": dma((6, 3)),
        "vs": dma((4, 3)), "vr": dma((4, 3)),
    }


def body(*refs):
    names = ["in_" + n for n in INPUTS] + ["out_" + n for n in OUTPUTS] + list(scratch())
    r = types.SimpleNamespace(**dict(zip(names, refs)))
    la = lax.axis_index("lat")
    lo = lax.axis_index("lon")
    me = la * 32 + lo
    z, y, x, c = la, lo // 8, lax.rem(lo // 2, 4), lax.rem(lo, 2)

    def at(z, y, x, c):
        return (z, y * 8 + x * 2 + c)

    coord = {"x": x, "y": y, "z": z}

    def peer(axis, d):
        p = dict(coord)
        p[axis] = lax.rem(coord[axis] + d, 4)
        return at(p["z"], p["y"], p["x"], c), p[axis]

    def rcopy(src, dst, ssem, rsem, device):
        return pltpu.make_async_remote_copy(src, dst, ssem, rsem, device_id=device, device_id_type=MESH)

    orders = {m: ("xyz", "yzx", "zxy")[m % 3] for m in range(6)}
    scale = float(ROWS * DEVICES) ** -0.5
    other = at(z, y, x, 1 - c)

    def half(core):
        return pl.ds(pl.multiple_of(core * 256, 256), 256)

    def core_copy(m):
        return rcopy(r.part.at[m, half(1 - c)], r.crecv.at[m], r.cs.at[m], r.cr.at[m], other)

    def rs1(m, d):
        device, pos = peer(orders[m][0], d)
        rows = pl.ds(pl.multiple_of(pos * 64, 64), 64)
        return rcopy(r.s1.at[m, rows], r.r1.at[m, d - 1], r.s1s.at[m, d - 1], r.s1r.at[m, d - 1], device)

    def rs2(m, d):
        device, pos = peer(orders[m][1], d)
        rows = pl.ds(pl.multiple_of(pos * 16, 16), 16)
        return rcopy(r.s2.at[m, rows], r.r2.at[m, d - 1], r.s2s.at[m, d - 1], r.s2r.at[m, d - 1], device)

    def swap3(m, d):
        device, _ = peer(orders[m][2], d)
        return rcopy(r.r3.at[m, 0], r.r3.at[m, d], r.s3s.at[m, d - 1], r.s3r.at[m, d - 1], device)

    def spot(m, level):
        a, b = coord[orders[m][0]] * 64, coord[orders[m][1]] * 16
        if level == 2:
            return r.res.at[m, pl.ds(pl.multiple_of(c * 256 + a + b, 16), 16)]
        if level == 1:
            return r.res.at[m, pl.ds(pl.multiple_of(c * 256 + a, 64), 64)]
        return r.res.at[m, half(c)]

    def ag(m, level, d):
        ssem, rsem = {2: (r.g2s, r.g2r), 1: (r.g1s, r.g1r)}[level]
        device, _ = peer(orders[m][level - 1], d)
        return rcopy(spot(m, level), spot(m, level), ssem.at[m, d - 1], rsem.at[m, d - 1], device)

    def ag_core(m):
        return rcopy(spot(m, 0), spot(m, 0), r.gcs.at[m], r.gcr.at[m], other)

    def fold_core(m):
        core_copy(m).wait()
        r.s1[m] = (r.part[m, half(c)].astype(F32) + r.crecv[m].astype(F32)).astype(BF16)
        for d in (2, 1, 3):
            rs1(m, d).start()

    def fold1(m):
        total = r.s1[m, pl.ds(pl.multiple_of(coord[orders[m][0]] * 64, 64), 64)].astype(F32)
        for d in (1, 3, 2):
            rs1(m, d).wait()
            total += r.r1[m, d - 1].astype(F32)
        r.s2[m] = total.astype(BF16)
        for d in (2, 1, 3):
            rs2(m, d).start()

    def fold2(m):
        total = r.s2[m, pl.ds(pl.multiple_of(coord[orders[m][1]] * 16, 16), 16)].astype(F32)
        for d in (1, 3, 2):
            rs2(m, d).wait()
            total += r.r2[m, d - 1].astype(F32)
        r.r3[m, 0] = total.astype(BF16)
        for d in (2, 1, 3):
            swap3(m, d).start()

    def fold3(m):
        for d in (1, 3, 2):
            swap3(m, d).wait()
        total = jnp.zeros((16, D), F32)
        for i in range(4):
            total += r.r3[m, lax.rem(coord[orders[m][2]] - i + 4, 4)].astype(F32)
        spot(m, 2)[...] = (total * scale).astype(BF16)
        for d in (2, 1, 3):
            ag(m, 2, d).start()

    def spread(m, level):
        for d in (1, 3, 2):
            ag(m, level, d).wait()
        if level == 2:
            for d in (2, 1, 3):
                ag(m, 1, d).start()
        else:
            ag_core(m).start()
            store(r.res.at[m, half(c)], r.out_res.at[m, half(c)])

    def vec_copies(level):
        if level == 0:
            return [rcopy(r.vec.at[0], r.vrecv.at[0, 1], r.vs.at[0, 0], r.vr.at[0, 0], other)]
        return [
            rcopy(r.vec.at[level], r.vrecv.at[level, d], r.vs.at[level, d - 1], r.vr.at[level, d - 1], peer("xyz"[level - 1], d)[0])
            for d in (1, 2, 3)
        ]

    def vec_step(level):
        for q in vec_copies(level):
            q.wait()
        if level == 0:
            total = r.vec[0] + r.vrecv[0, 1]
        else:
            r.vrecv[level, 0] = r.vec[level]
            total = jnp.zeros((8, D), F32)
            for i in range(4):
                total += r.vrecv[level, lax.rem(coord["xyz"[level - 1]] - i + 4, 4)]
        if level < 3:
            r.vec[level + 1] = total
            for q in vec_copies(level + 1):
                q.start()
        else:
            r.vout[...] = total[0:4] * scale
            store(r.vout, r.out_vout)

    bar = pltpu.get_barrier_semaphore()

    zs = [lax.rem(z + i, 4) for i in range(4)]
    ys = [lax.rem(y + i, 4) * 8 for i in range(4)]
    xs = [lax.rem(x + i, 4) * 2 for i in range(4)]
    cores = [c, 1 - c]

    def away(d):
        return (zs[d[0]], ys[d[1]] + xs[d[2]] + cores[d[3]])

    for d in ORDER:
        pl.semaphore_signal(bar, inc=1, device_id=away(d), device_id_type=MESH)

    def load(name):
        return pltpu.make_async_copy(getattr(r, "in_" + name), getattr(r, name), r.loads.at[INPUTS.index(name)])

    def need(*wanted):
        for name in wanted:
            load(name).wait()

    stores = []

    def store(source, target):
        copy = pltpu.make_async_copy(source, target, r.stores.at[len(stores)])
        copy.start()
        stores.append(copy)

    for name in ("lat", "ngain", "csend", "near", "slot", "rw", "ebias", "sw", "cot", "no", "ni", "nbias", "ew", "egain"):
        load(name).start()
    need("lat", "ngain", "csend", "near", "slot")

    h, inv = norm_rows(r.lat[...].astype(F32))
    r.lhat[...] = h
    r.linv[...] = inv
    r.ext_n[RIM : RIM + ROWS] = (h * r.ngain[...]).astype(BF16)

    idx = jnp.concatenate([r.near[...], r.slot[...], jnp.zeros((2, ROWS), jnp.int32)], axis=0)
    idx_t = jnp.transpose(idx)
    for k in range(EDGES):
        r.cols[k] = idx_t[:, k : k + 1]
    send_t = jnp.transpose(r.csend[...].reshape(8, 128))
    for j in range(8):
        rows = mm(lane_hot(send_t[:, j : j + 1], ROWS), r.ext_n[RIM : RIM + ROWS])
        r.pk[16 * j : 16 * j + 16] = to_pairs(rows)

    pl.semaphore_wait(bar, DEVICES - 1)

    west = (la, lax.rem(lo + 31, 32))
    east = (la, lax.rem(lo + 1, 32))
    halo = [
        rcopy(r.ext_n.at[pl.ds(2 * RIM, RIM)], r.ext_n.at[pl.ds(0, RIM)], r.hs.at[0], r.hr.at[0], east),
        rcopy(r.ext_n.at[pl.ds(RIM, RIM)], r.ext_n.at[pl.ds(3 * RIM, RIM)], r.hs.at[1], r.hr.at[1], west),
    ]
    for q in halo:
        q.start()

    for d in ORDER:
        t = away(d)
        rcopy(r.pk.at[t[0] * 32 + t[1]], r.arr.at[me], r.as_, r.ar, t).start()

    r.arr[me] = r.pk[me]

    need("rw", "ebias", "sw", "cot", "no", "ni", "nbias", "ew", "egain")

    def own():
        return r.ext_n[RIM : RIM + ROWS]

    r.recv[...] = mm(own(), r.rw[...]) + r.ebias[...]
    r.sent_ext[RIM : RIM + ROWS] = mm(own(), r.sw[...]).astype(BF16)
    r.gh[...] = mm_bt(r.cot[...], r.no[...])
    r.npre[...] = mm(own(), r.ni[0:D]) + r.nbias[...]
    r.hsum[...] = jnp.zeros((ROWS, D), F32)
    for q in halo:
        q.wait()
    r.sent_ext[0:RIM] = mm(r.ext_n[0:RIM], r.sw[...]).astype(BF16)
    r.sent_ext[3 * RIM : 4 * RIM] = mm(r.ext_n[3 * RIM : 4 * RIM], r.sw[...]).astype(BF16)

    def edge_forward(k, senders):
        a, s = silu_parts(senders + r.recv[...])
        a = a.astype(BF16)
        r.act[k] = a
        r.slope[k] = s
        h, inv = norm_rows(mm(a, r.ew[...]))
        r.hat[k] = h
        r.einv[k] = inv
        r.hsum[...] += h

    @pl.loop(0, DEG)
    def _(k):
        edge_forward(k, mm(lane_hot(r.cols[k], ROWS + 2 * RIM), r.sent_ext[...]))

    everything = rcopy(r.pk.at[pl.ds(0, DEVICES - 1)], r.arr.at[pl.ds(0, DEVICES - 1)], r.as_, r.ar, west)
    everything.wait()

    @pl.loop(0, 8)
    def _(j):
        r.arr_n[pl.ds(pl.multiple_of(j * 128, 128), 128)] = from_pairs(r.arr[pl.ds(j * 16, 16)])

    @pl.loop(0, CDEG)
    def _(k):
        rows = mm(lane_hot(r.cols[DEG + k], SLOTS), r.arr_n[...]).astype(BF16)
        r.ext_n[pl.ds(pl.multiple_of(EXT + k * ROWS, ROWS), ROWS)] = rows
        edge_forward(DEG + k, mm(rows, r.sw[...]).astype(BF16).astype(F32))

    aggregate = (r.hsum[...] * r.egain[...]).astype(BF16)
    hidden, node_slope = silu_parts(r.npre[...] + mm(aggregate, r.ni[D : 2 * D]))
    hidden = hidden.astype(BF16)
    r.hidden[...] = hidden
    gnp = (r.gh[...] * node_slope).astype(BF16)
    r.gnp[...] = gnp
    r.aggr[...] = aggregate
    gagg = mm_bt(gnp, r.ni[D : 2 * D])
    r.vec[0] = jnp.zeros((8, D), F32)
    r.vec[0, 2:3] = col_sum(gagg * r.hsum[...])
    r.vec[0, 3:4] = col_sum(gnp.astype(F32))
    r.part[NODE_OUT] = mm_at(r.hidden[...], r.cot[...]).astype(BF16)
    r.part[NODE_SELF] = mm_at(own(), r.gnp[...]).astype(BF16)

    r.part[NODE_AGG] = mm_at(r.aggr[...], r.gnp[...]).astype(BF16)
    early, late = (NODE_OUT, NODE_SELF, NODE_AGG), (RECEIVE, EDGE, SEND)
    for m in early:
        core_copy(m).start()

    up = gagg * r.egain[...]
    r.npre[...] = up - mean_row(up)
    r.gh[...] = up

    def edge_backward(k):
        h = r.hat[k]
        g = (r.einv[k] * (r.npre[...] - h * mean_row(r.gh[...] * h))).astype(BF16)
        ge = mm_bt(g, r.ew[...]) * r.slope[k]
        r.gpre[k] = g
        return ge

    total = jnp.zeros((ROWS, D), F32)
    for k in range(CDEG):
        ge = edge_backward(DEG + k)
        total += ge
        r.gsend[EXT + k * ROWS : EXT + (k + 1) * ROWS] = ge.astype(BF16)
    r.recv[...] = total
    for j in range(4):
        block = jnp.zeros((256, D), F32)
        for k in range(CDEG):
            block += mm(sub_hot(r.slot[k : k + 1, :] - 256 * j, 256), r.gsend[EXT + k * ROWS : EXT + (k + 1) * ROWS])
        r.pk2[32 * j : 32 * j + 32] = to_pairs(block)
    r.arr2[me] = r.pk2[me]

    def send_back(first, last):
        for d in ORDER[first:last]:
            t = away(d)
            rcopy(r.pk2.at[t[0] * 32 + t[1]], r.arr2.at[me], r.as2, r.ar2, t).start()

    send_back(0, FIRST)
    for m in early:
        fold_core(m)

    @pl.loop(0, DEG, step=2)
    def _(k):
        one, two = edge_backward(k), edge_backward(k + 1)
        r.geb[k] = one.astype(BF16)
        r.geb[k + 1] = two.astype(BF16)
        r.recv[...] += one + two

    flat = (EDGES * ROWS, D)
    r.part[EDGE] = mm_at(r.act[...].reshape(flat), r.gpre[...].reshape(flat)).astype(BF16)
    core_copy(EDGE).start()
    r.grecv[...] = r.recv[...].astype(BF16)
    r.part[RECEIVE] = mm_at(own(), r.grecv[...]).astype(BF16)
    core_copy(RECEIVE).start()
    for j in range(4):
        block = jnp.zeros((RIM, D), F32)
        for k in range(DEG):
            block += mm(sub_hot(r.near[k : k + 1, :] - RIM * j, RIM), r.geb[k])
        r.gext[RIM * j : RIM * j + RIM] = block
        r.gsend[RIM * j : RIM * j + RIM] = block.astype(BF16)
    r.acc[...] = mm_at(r.ext_n[...], r.gsend[...])
    r.part[SEND] = r.acc[...].astype(BF16)
    core_copy(SEND).start()
    for m in early:
        fold1(m)
    for m in (EDGE, RECEIVE, SEND):
        fold_core(m)

    halo_back = [
        rcopy(r.gsend.at[pl.ds(3 * RIM, RIM)], r.rims.at[0], r.hs2.at[0], r.hr2.at[0], east),
        rcopy(r.gsend.at[pl.ds(0, RIM)], r.rims.at[1], r.hs2.at[1], r.hr2.at[1], west),
    ]
    for q in halo_back:
        q.start()
    local_back = mm_bt(r.gnp[...], r.ni[0:D]) + mm_bt(r.grecv[...], r.rw[...])
    r.gnb[...] = local_back
    through_sent = jnp.sum(r.sw[...].astype(F32) * r.acc[...], axis=1, keepdims=True)
    through_sent = jnp.transpose(jnp.broadcast_to(through_sent, (D, 128)))[0:1]
    r.vec[0, 0:1] = col_sum(r.lhat[...] * local_back) + through_sent / r.ngain[...]
    r.vec[0, 1:2] = col_sum(r.recv[...])
    for q in vec_copies(0):
        q.start()

    for m in late:
        fold1(m)
    for m in early:
        fold2(m)
    r.newlat[...] = (r.lat[...].astype(F32) + mm(r.hidden[...], r.no[...])).astype(BF16)
    store(r.newlat, r.out_newlat)
    vec_step(0)
    send_back(FIRST, SECOND)
    for m in late:
        fold2(m)
    for m in early:
        fold3(m)
    vec_step(1)
    send_back(SECOND, THIRD)
    for m in late:
        fold3(m)
    for m in early:
        spread(m, 2)
    send_back(THIRD, DEVICES - 1)
    vec_step(2)
    for m in late:
        spread(m, 2)
    for m in early:
        spread(m, 1)
    vec_step(3)

    for q in halo_back:
        q.wait()
    grad_sent = r.gext[RIM : RIM + ROWS] + r.rims[...].reshape(ROWS, D).astype(F32)
    rcopy(r.pk2.at[pl.ds(0, DEVICES - 1)], r.arr2.at[pl.ds(0, DEVICES - 1)], r.as2, r.ar2, west).wait()

    @pl.loop(0, 8)
    def _(j):
        r.arr_n[pl.ds(pl.multiple_of(j * 128, 128), 128)] = from_pairs(r.arr2[pl.ds(j * 16, 16)])

    grad_sent += mm(sub_hot(r.csend[...], ROWS), r.arr_n[...])
    up = (r.gnb[...] + mm_bt(grad_sent.astype(BF16), r.sw[...])) * r.ngain[...]
    h = r.lhat[...]
    back = r.linv[...] * (up - mean_row(up) - h * mean_row(up * h))
    r.glat[...] = (r.cot[...].astype(F32) + back).astype(BF16)
    store(r.glat, r.out_glat)

    for m in late:
        spread(m, 1)
    for m in range(6):
        ag_core(m).wait()
        store(r.res.at[m, half(1 - c)], r.out_res.at[m, half(1 - c)])
    for copy in stores:
        copy.wait()


def widen(sums, newlat, glat, vectors, *refs):
    outs, narrow, wide, rows, vec, in_sems, out_sems = refs[:8], *refs[8:]
    loads = [pltpu.make_async_copy(sums.at[m], narrow.at[m], in_sems.at[m]) for m in range(6)]
    through = ((newlat, rows.at[0], outs[0]), (glat, rows.at[1], outs[1]), (vectors, vec, outs[7]))
    for i, (source, held, _) in enumerate(through):
        loads.append(pltpu.make_async_copy(source, held, in_sems.at[6 + i]))
    for copy in loads:
        copy.start()
    stores = []

    def store(source, target):
        copy = pltpu.make_async_copy(source, target, out_sems.at[len(stores)])
        copy.start()
        stores.append(copy)

    targets = {
        SEND: outs[2], RECEIVE: outs[3], EDGE: outs[4], NODE_OUT: outs[6],
        NODE_SELF: outs[5].at[pl.ds(0, D)], NODE_AGG: outs[5].at[pl.ds(D, D)],
    }
    for m in range(6):
        loads[m].wait()
        wide[m] = narrow[m].astype(F32)
        store(wide.at[m], targets[m])
    for i, (_, held, target) in enumerate(through):
        loads[6 + i].wait()
        store(held, target)
    for copy in stores:
        copy.wait()


def per_device(
    latents, near_index, coarse_slot, coarse_send, norm_gain, send_weight, receive_weight, edge_bias,
    edge_weight, edge_gain, node_input, node_bias, node_output, cotangent,
):
    whole = pl.BlockSpec(memory_space=pltpu.HBM)
    new_latents, grad_latents, sums, vectors = pl.pallas_call(
        body,
        out_shape=(
            jax.ShapeDtypeStruct((ROWS, D), BF16),
            jax.ShapeDtypeStruct((ROWS, D), BF16),
            jax.ShapeDtypeStruct((6, D, D), BF16),
            jax.ShapeDtypeStruct((4, D), F32),
        ),
        in_specs=[whole] * 14,
        out_specs=(whole,) * 4,
        scratch_shapes=list(scratch().values()),
        compiler_params=pltpu.CompilerParams(
            collective_id=0, has_side_effects=True, vmem_limit_bytes=58 * 2**20
        ),
    )(
        latents, near_index, coarse_slot, coarse_send, norm_gain.reshape(1, D), send_weight, receive_weight,
        edge_bias.reshape(1, D), edge_weight, edge_gain.reshape(1, D), node_input, node_bias.reshape(1, D),
        node_output, cotangent,
    )
    shard, one = jax.ShapeDtypeStruct((ROWS, D), BF16), jax.ShapeDtypeStruct((D, D), F32)
    return pl.pallas_call(
        widen,
        out_shape=(
            shard, shard, one, one, one, jax.ShapeDtypeStruct((2 * D, D), F32), one,
            jax.ShapeDtypeStruct((4, D), F32),
        ),
        in_specs=[whole] * 4,
        out_specs=(whole,) * 8,
        scratch_shapes=[
            pltpu.VMEM((6, D, D), BF16), pltpu.VMEM((6, D, D), F32),
            pltpu.VMEM((2, ROWS, D), BF16), pltpu.VMEM((4, D), F32),
            pltpu.SemaphoreType.DMA((9,)), pltpu.SemaphoreType.DMA((9,)),
        ],
        compiler_params=pltpu.CompilerParams(vmem_limit_bytes=58 * 2**20),
    )(sums, new_latents, grad_latents, vectors)


def solution(mesh):
    rows, whole = P(("lat", "lon"), None), P()
    split = P(None, ("lat", "lon"))
    return jax.shard_map(
        per_device,
        mesh=mesh,
        in_specs=(rows, split, split, rows) + (whole,) * 9 + (rows,),
        out_specs=(rows, rows) + (whole,) * 6,
        check_vma=False,
    )
```
